128 devices in a mesh: pair: 4 (over z), virt: 32 (over y, x, core).
Axes of the slice: x: 4, y: 4, z: 4, core: 2. Of those that a mesh axis runs over, the one named last changes fastest.
Arguments:
- amps: bfloat16 [16, 768, 768], P('pair', 'virt'), may hold values from -6 to 6
- domain: int32 [16, 6], replicated, may hold values from 0 to 31, as said below
- pair_mask: int32 [16, 6, 6], P('pair'), may hold values 0 or 1
- dfint: bfloat16 [32, 4096, 4096], P('virt', 'pair'), may hold values from -0.09375 to 0.09375
- coupling: float32 [16, 16], P('pair'), may hold values from -1.75 to 1.75
Outputs:
- residual: bfloat16 [16, 768, 768], P('pair', 'virt')
The draws below stay inside these ranges and needn't reach their ends.
Inputs may be any that keep to these rules, and one draw needn't show every extreme that they name: `domain`: each row lists 6 different tiles; of the 4 blocks of 8 consecutive tiles, none holds more than 2 tiles of one row, and some block holds exactly 2.
All inputs are finite; a program needn't handle non-finite values. No bound on the sum of `pair_mask` on one device may be relied on, other than what follows from the above.
Results may differ from the reference program's by a relative error of at most 0.0038.
Values may be sent and summed in bfloat16 or wider, within the bound.
No kernel may reach another device: no remote copies, remote signals or barrier semaphores. Data moves between devices by JAX's collectives and lax.ppermute only.
A program may use at most 192 MiB of HBM per device.

```python
import jax
import jax.numpy as jnp
from jax import lax

TB = 128
TILES = 32
DOM = 6
CAP = 2
AUX = 32
PAIRS = 16
V = 4096
N_PAIR = 4


def draw_domain(key, part):
    key = jax.random.fold_in(key, 11)
    quart = TILES // N_PAIR
    base = jnp.clip(DOM - CAP * jnp.arange(N_PAIR, dtype=jnp.int32), 0, CAP).astype(jnp.int32)

    def one_pair(pair_key):
        flag_key, order_key, inner_key, list_key = jax.random.split(pair_key, 4)
        flag = jax.random.randint(flag_key, (), 0, 2).astype(jnp.int32)
        shifted = base.at[0].add(-flag).at[N_PAIR - 1].add(flag)
        counts = shifted[jax.random.permutation(order_key, N_PAIR)]
        ranks = jax.vmap(lambda one_key: jax.random.permutation(one_key, quart))(jax.random.split(inner_key, N_PAIR))
        selected = (ranks < counts[:, None]).reshape(TILES)
        order_ranks = jax.random.permutation(list_key, TILES).astype(jnp.int32)
        scores = jnp.where(selected, order_ranks, TILES + jnp.arange(TILES, dtype=jnp.int32))
        return jnp.argsort(scores)[:DOM].astype(jnp.int32)
    return jax.vmap(one_pair)(jax.random.split(key, PAIRS))


def with_ends(entries, rng, low, top_value):
    longest = entries.shape.index(max(entries.shape))
    spots = []
    for shift in (0, 1):
        where = [jax.random.randint(jax.random.fold_in(rng, axis), (), 0, length) for axis, length in enumerate(entries.shape)]
        where[longest] = (where[longest] + shift) % entries.shape[longest]
        spots.append(tuple(where))
    return entries.at[spots[0]].set(low).at[spots[1]].set(top_value)


def level_of(key, shape, shards, low, largest):
    factor_of = 1.0
    for dim, blocks in shards:
        draws = jax.random.uniform(jax.random.fold_in(jax.random.fold_in(key, 6), dim), (blocks,), jnp.float32, low / len(shards), largest / len(shards))
        factor_of = factor_of * jnp.repeat(jnp.exp(draws), shape[dim] // blocks).reshape((-1,) + (1,) * (len(shape) - 1 - dim))
    return factor_of


def scatter_about(key, dims, scale, reach, cuts=(), kind=jnp.bfloat16):
    array = jax.random.normal(key, dims, jnp.float32) * scale
    if len(cuts) > 0:
        array = level_of(key, dims, cuts, -0.22, 0.18) * array
    return jnp.clip(array, min=-reach, max=reach).astype(kind)


def setup_inputs(seed: int = 0) -> dict:
    keys = jax.random.split(jax.random.key(seed), 6)
    return {
        "amps": scatter_about(keys[0], (PAIRS, DOM * TB, DOM * TB), 1.0, 6.0, ((0, 4), (1, 32))),
        "domain": draw_domain(jax.random.fold_in(keys[5], 71), 0),
        "pair_mask": with_ends((jax.random.randint(keys[2], (PAIRS, DOM, DOM), 0, 4) < 3).astype(jnp.int32), jax.random.fold_in(keys[2], 1), 0, 1),
        "dfint": scatter_about(keys[3], (AUX, V, V), (DOM * TB * 6) ** -0.5, 0.09375, ((0, 32), (1, 4))),
        "coupling": scatter_about(keys[4], (PAIRS, PAIRS), 0.3, 1.75, ((0, 4),), jnp.float32),
    }


def pick_tiles(square, tiles_of_pair):
    leading = square.shape[:-2]
    blocks = square.reshape(leading + (TILES, TB, TILES, TB))
    row_tiles = jnp.take(blocks, tiles_of_pair, axis=-4)
    both_tiles = jnp.take(row_tiles, tiles_of_pair, axis=-2)
    return both_tiles.reshape(leading + (DOM * TB, DOM * TB))


def reference(amps, domain, pair_mask, dfint, coupling):
    high = lax.Precision.HIGHEST
    tile_mask = jnp.repeat(jnp.repeat(pair_mask, TB, axis=1), TB, axis=2).astype(jnp.bfloat16)
    amp_block = amps * tile_mask

    def intersection_of(items):
        amp_one, tiles_of_pair = items
        int_wide = pick_tiles(dfint, tiles_of_pair).astype(jnp.float32)
        return jnp.einsum('qab,ab->q', int_wide, amp_one.astype(jnp.float32), precision=high)

    intersections = lax.map(intersection_of, (amp_block, domain))
    dressing = jnp.dot(coupling, intersections, precision=high)

    def combine(items):
        amp_one, tiles_of_pair, dress_one = items
        int_wide = pick_tiles(dfint, tiles_of_pair).astype(jnp.float32)
        amp_wide = amp_one.astype(jnp.float32)
        half_ladder = jnp.einsum('qbd,cd->qbc', int_wide, amp_wide, precision=high).astype(jnp.bfloat16)
        ladder = jnp.einsum('qac,qbc->ab', int_wide, half_ladder.astype(jnp.float32), precision=high)
        cycle_term = jnp.einsum('q,qab->ab', dress_one, int_wide, precision=high)
        return (ladder + cycle_term).astype(jnp.bfloat16)

    return lax.map(combine, (amp_block, domain, dressing))
```

```python
import functools

import jax
import jax.numpy as jnp
from jax import lax
from jax.experimental import pallas as pl
from jax.experimental.pallas import tpu as pltpu
from jax.sharding import Mesh
from jax.sharding import PartitionSpec as P

TB = 128
BLOCKS = 4
SLOTS = 2
BF16 = jnp.bfloat16
F32 = jnp.float32
NT = (((1,), (1,)), ((), ()))


def ring(axis, shift, size):
    return functools.partial(
        lax.ppermute, axis_name=axis, perm=[(i, (i + shift) % size) for i in range(size)]
    )


def block_slots(domain_ref, pair, block, quarter, dom):
    found = jnp.int32(0)
    first = jnp.int32(0)
    second = jnp.int32(0)
    for s in range(dom):
        inside = domain_ref[pair, s] // quarter == block
        first = jnp.where(inside & (found == 0), s, first)
        second = jnp.where(inside & (found == 1), s, second)
        found = found + inside.astype(jnp.int32)
    return first, second


def pack_kernel(quarter, dom, domain_ref, here_ref, dfint_ref, *out_and_sem):
    outs, sem = out_and_sem[:-1], out_and_sem[-1]
    here = here_ref[0]
    pairs = outs[0].shape[0]
    for shift in (1, 2, 3, 0):
        target = lax.rem(here + shift, BLOCKS)

        def one_pair(k, carry):
            pair = target * pairs + k
            for j, slot in enumerate(block_slots(domain_ref, pair, here, quarter, dom)):
                row = jnp.clip(domain_ref[pair, slot] - here * quarter, 0, quarter - 1)
                for t in range(dom):
                    column = domain_ref[pair, t]
                    pltpu.make_async_copy(
                        dfint_ref.at[
                            0,
                            pl.ds(pl.multiple_of(row * TB, TB), TB),
                            pl.ds(pl.multiple_of(column * TB, TB), TB),
                        ],
                        outs[shift].at[k, j, :, pl.ds(t * TB, TB)],
                        sem.at[shift],
                    ).start()
            return carry

        lax.fori_loop(0, pairs, one_pair, 0)
    for shift in range(BLOCKS):
        pltpu.make_async_copy(outs[shift], outs[shift], sem.at[shift]).wait()


def pack(dfint, domain, here, pairs, quarter):
    dom = domain.shape[1]
    out = jax.ShapeDtypeStruct((pairs, SLOTS, TB, dom * TB), BF16)
    return pl.pallas_call(
        functools.partial(pack_kernel, quarter, dom),
        out_shape=[out] * BLOCKS,
        grid_spec=pltpu.PrefetchScalarGridSpec(
            num_scalar_prefetch=2,
            grid=(1,),
            in_specs=[pl.BlockSpec(memory_space=pl.ANY)],
            out_specs=[pl.BlockSpec(memory_space=pl.ANY)] * BLOCKS,
            scratch_shapes=[pltpu.SemaphoreType.DMA((BLOCKS,))],
        ),
        name="pack_tiles",
    )(domain, here, dfint)


def fetch_rows(quarter, dom, domain_ref, here, k, pairs, parts, block, sem):
    pair = here * pairs + k
    for s in range(dom):
        owner = domain_ref[pair, s] // quarter
        rank = jnp.int32(0)
        for before in range(s):
            rank = rank + (domain_ref[pair, before] // quarter == owner).astype(jnp.int32)
        shift = lax.rem(here - owner + BLOCKS, BLOCKS)
        for option in range(BLOCKS):

            @pl.when(shift == option)
            def _(option=option):
                pltpu.make_async_copy(
                    parts[option].at[k, rank], block.at[k, pl.ds(s * TB, TB), :], sem.at[k]
                ).start()


def gather_start(quarter, dom, domain_ref, here, parts, block, sem):
    pairs = block.shape[0]

    @pl.when(pl.program_id(0) == 0)
    def _():
        for k in range(pairs):
            fetch_rows(quarter, dom, domain_ref, here, k, pairs, parts, block, sem)

    k = pl.program_id(0)
    pltpu.make_async_copy(block.at[k], block.at[k], sem.at[k]).wait()


def half_kernel(quarter, dom, domain_ref, here_ref, amp_ref, p0, p1, p2, p3, half_ref, inter_ref, block, sem):
    k = pl.program_id(0)
    gather_start(quarter, dom, domain_ref, here_ref[0], (p0, p1, p2, p3), block, sem)
    amp = amp_ref[0]
    total = jnp.float32(0)
    rows = 2 * TB
    for r in range(0, dom * TB, rows):
        half = lax.dot_general(block[k, pl.ds(r, rows), :], amp, NT, preferred_element_type=F32)
        half_ref[0, pl.ds(r, rows), :] = half.astype(BF16)
        corner = half[:, r : r + rows]
        diagonal = lax.broadcasted_iota(jnp.int32, (rows, rows), 0) == lax.broadcasted_iota(
            jnp.int32, (rows, rows), 1
        )
        total = total + jnp.sum(jnp.where(diagonal, corner, 0.0))
    inter_ref[0, k] = total


def half_ladders(amp, parts, domain, here, quarter):
    pairs, length = amp.shape[0], amp.shape[1]
    dom = domain.shape[1]
    return pl.pallas_call(
        functools.partial(half_kernel, quarter, dom),
        out_shape=[
            jax.ShapeDtypeStruct((pairs, length, length), BF16),
            jax.ShapeDtypeStruct((1, pairs), F32),
        ],
        grid_spec=pltpu.PrefetchScalarGridSpec(
            num_scalar_prefetch=2,
            grid=(pairs,),
            in_specs=[pl.BlockSpec((1, length, length), lambda k, *_: (k, 0, 0))]
            + [pl.BlockSpec(memory_space=pl.ANY)] * BLOCKS,
            out_specs=[
                pl.BlockSpec((1, length, length), lambda k, *_: (k, 0, 0)),
                pl.BlockSpec(memory_space=pltpu.SMEM),
            ],
            scratch_shapes=[
                pltpu.VMEM((pairs, length, length), BF16),
                pltpu.SemaphoreType.DMA((pairs,)),
            ],
        ),
        compiler_params=pltpu.CompilerParams(vmem_limit_bytes=40 * 2**20),
        name="half_ladder",
    )(domain, here, amp, *parts)


def ladder_kernel(
    quarter, dom, ny, nx, domain_ref, here_ref, coupling_ref, i0, i1, i2, i3, half_ref, p0, p1, p2, p3,
    keep_ref, send_ref, block, sem,
):
    k = pl.program_id(0)
    pairs = block.shape[0]
    here, y, x, core = here_ref[0], here_ref[1], here_ref[2], here_ref[3]
    gather_start(quarter, dom, domain_ref, here, (p0, p1, p2, p3), block, sem)
    dressing = jnp.float32(0)
    for shift, inter in enumerate((i0, i1, i2, i3)):
        owner = lax.rem(here - shift + BLOCKS, BLOCKS)
        for other in range(pairs):
            dressing = dressing + coupling_ref[k, owner * pairs + other] * inter[0, other]
    half = half_ref[0]
    own = keep_ref.shape[3]
    groups = 2 * nx
    rows = groups * own
    for yy in range(ny):
        mine = block[k, pl.ds(yy * rows, rows), :]
        acc = lax.dot_general(mine, half, NT, preferred_element_type=F32)
        acc = acc + dressing * mine.astype(F32)
        sy = lax.rem(yy - y + ny, ny)
        for xx in range(nx):
            sx = lax.rem(xx - x + nx, nx)
            low = acc[(2 * xx) * own : (2 * xx + 1) * own]
            high = acc[(2 * xx + 1) * own : (2 * xx + 2) * own]
            keep_ref[0, sy, sx] = jnp.where(core == 0, low, high)
            send_ref[0, sy, sx] = jnp.where(core == 0, high, low).astype(BF16)


def ladders(half, parts, inters, coupling, domain, here, quarter, ny, nx, own):
    pairs, length = half.shape[0], half.shape[1]
    dom = domain.shape[1]
    shape = (pairs, ny, nx, own, length)
    spec = pl.BlockSpec((1,) + shape[1:], lambda k, *_: (k, 0, 0, 0, 0))
    smem = pl.BlockSpec(memory_space=pltpu.SMEM)
    return pl.pallas_call(
        functools.partial(ladder_kernel, quarter, dom, ny, nx),
        out_shape=[jax.ShapeDtypeStruct(shape, F32), jax.ShapeDtypeStruct(shape, BF16)],
        grid_spec=pltpu.PrefetchScalarGridSpec(
            num_scalar_prefetch=2,
            grid=(pairs,),
            in_specs=[smem] * 5
            + [pl.BlockSpec((1, length, length), lambda k, *_: (k, 0, 0))]
            + [pl.BlockSpec(memory_space=pl.ANY)] * BLOCKS,
            out_specs=[spec, spec],
            scratch_shapes=[
                pltpu.VMEM((pairs, length, length), BF16),
                pltpu.SemaphoreType.DMA((pairs,)),
            ],
        ),
        compiler_params=pltpu.CompilerParams(vmem_limit_bytes=40 * 2**20),
        name="ladder_and_cycle",
    )(domain, here, coupling, *inters, half, *parts)


def masked_amps(amps, pair_mask, first_row, dom):
    pairs, rows, length = amps.shape
    row_slot = (first_row + jnp.arange(rows, dtype=jnp.int32)) // TB
    slot_pick = row_slot[:, None] == jnp.arange(dom, dtype=jnp.int32)[None, :]
    row_tiles = jnp.sum(
        jnp.where(slot_pick[None, :, :, None], pair_mask[:, None, :, :], 0), axis=2
    ).astype(BF16)
    tiles = amps.reshape(pairs, rows, dom, TB) * row_tiles[:, :, :, None]
    return tiles.reshape(pairs, rows, length)


def make_body(ny, nx):
    def body(amps, domain, pair_mask, dfint, coupling):
        pairs, own, length = amps.shape
        dom = domain.shape[1]
        quarter = dfint.shape[1] // TB
        z, y, x, c = (lax.axis_index(name).astype(jnp.int32) for name in ("z", "y", "x", "c"))
        here = jnp.stack([z, y, x, c])
        packed = pack(dfint, domain, here, pairs, quarter)
        parts = [packed[0]] + [ring("z", s, BLOCKS)(packed[s]) for s in (1, 2, 3)]
        first_row = ((y * nx + x) * 2 + c) * own
        masked = masked_amps(amps, pair_mask, first_row, dom)
        amp = lax.all_gather(masked, ("y", "x", "c"), axis=1, tiled=True)
        half, inter = half_ladders(amp, parts, domain, here, quarter)
        inters = [inter] + [ring("z", s, BLOCKS)(inter) for s in (1, 2, 3)]
        keep, send = ladders(half, parts, inters, coupling, domain, here, quarter, ny, nx, own)
        summed = keep + ring("c", 1, 2)(send).astype(F32)
        cut = pairs // 2
        ends = []
        for part, axes in ((summed[:cut], "xy"), (summed[cut:], "yx")):
            first = part if axes == "xy" else jnp.swapaxes(part, 1, 2)
            n1, n2 = (nx, ny) if axes == "xy" else (ny, nx)
            stage = first[:, :, 0]
            for s in range(1, n1):
                stage = stage + ring(axes[0], s, n1)(first[:, :, s].astype(BF16)).astype(F32)
            last = stage[:, 0]
            for s in range(1, n2):
                last = last + ring(axes[1], s, n2)(stage[:, s].astype(BF16)).astype(F32)
            ends.append(last)
        return jnp.concatenate(ends, axis=0).astype(BF16)

    return body


def solution(mesh):
    ny = nx = 4
    grid = Mesh(mesh.devices.reshape(BLOCKS, ny, nx, 2), ("z", "y", "x", "c"))
    virt = ("y", "x", "c")
    return jax.shard_map(
        make_body(ny, nx),
        mesh=grid,
        in_specs=(P("z", virt, None), P(), P("z", None, None), P(virt, "z", None), P("z", None)),
        out_specs=P("z", virt, None),
        check_vma=False,
    )
```

```python
import functools

import jax
import jax.numpy as jnp
from jax import lax
from jax.experimental import pallas as pl
from jax.experimental.pallas import tpu as pltpu
from jax.sharding import Mesh
from jax.sharding import PartitionSpec as P

TB = 128
BLOCKS = 4
CORES = 2
SLOTS = 2
BF16 = jnp.bfloat16
F32 = jnp.float32
NT = (((1,), (1,)), ((), ()))
FLOWS = ((1, 0), (3, 0), (1, 1), (3, 1), (2, 0), (2, 1), (0, 1), (0, 0))


def hop(shift, flip):
    perm = [
        (z * CORES + c, (z + shift) % BLOCKS * CORES + (c ^ flip))
        for z in range(BLOCKS)
        for c in range(CORES)
    ]
    return functools.partial(lax.ppermute, axis_name=("z", "c"), perm=perm)


def swap_cores(value):
    return lax.ppermute(value, "c", [(0, 1), (1, 0)])


def block_slots(domain_ref, pair, block, quarter, dom):
    found = jnp.int32(0)
    first = jnp.int32(0)
    second = jnp.int32(0)
    for s in range(dom):
        inside = domain_ref[pair, s] // quarter == block
        first = jnp.where(inside & (found == 0), s, first)
        second = jnp.where(inside & (found == 1), s, second)
        found = found + inside.astype(jnp.int32)
    return first, second


def pack_kernel(quarter, dom, which, domain_ref, here_ref, dfint_ref, *rest):
    count = len(FLOWS)
    outs, (buffer, in_sem, out_sem) = rest[:count], rest[count:]
    here, core = here_ref[0], here_ref[3]
    for flow, (shift, flip) in enumerate(FLOWS):
        target = lax.rem(here + shift, BLOCKS)
        pair = (target * CORES + (core ^ flip)) * CORES + which
        for j, slot in enumerate(block_slots(domain_ref, pair, here, quarter, dom)):
            row = jnp.clip(domain_ref[pair, slot] - here * quarter, 0, quarter - 1)
            for t in range(dom):
                column = domain_ref[pair, t]
                pltpu.make_async_copy(
                    dfint_ref.at[
                        0,
                        pl.ds(pl.multiple_of(row * TB, TB), TB),
                        pl.ds(pl.multiple_of(column * TB, TB), TB),
                    ],
                    buffer.at[flow, j, :, pl.ds(t * TB, TB)],
                    in_sem.at[flow],
                ).start()
    for flow in range(count):
        pltpu.make_async_copy(buffer.at[flow], buffer.at[flow], in_sem.at[flow]).wait()
        pltpu.make_async_copy(buffer.at[flow], outs[flow], out_sem.at[flow]).start()
    for flow in range(count):
        pltpu.make_async_copy(buffer.at[flow], outs[flow], out_sem.at[flow]).wait()


def pack(dfint, domain, here, which, quarter):
    dom = domain.shape[1]
    count = len(FLOWS)
    tile_rows = (SLOTS, TB, dom * TB)
    return pl.pallas_call(
        functools.partial(pack_kernel, quarter, dom, which),
        out_shape=[jax.ShapeDtypeStruct(tile_rows, BF16)] * count,
        grid_spec=pltpu.PrefetchScalarGridSpec(
            num_scalar_prefetch=2,
            grid=(1,),
            in_specs=[pl.BlockSpec(memory_space=pl.ANY)],
            out_specs=[pl.BlockSpec(memory_space=pl.ANY)] * count,
            scratch_shapes=[
                pltpu.VMEM((count,) + tile_rows, BF16),
                pltpu.SemaphoreType.DMA((count,)),
                pltpu.SemaphoreType.DMA((count,)),
            ],
        ),
        compiler_params=pltpu.CompilerParams(vmem_limit_bytes=16 * 2**20),
        cost_estimate=pl.CostEstimate(flops=0, bytes_accessed=13 * 2**20, transcendentals=0),
        name="pack_tiles",
    )(domain, here, dfint)


def ladder_kernel(quarter, dom, which, domain_ref, here_ref, amp_ref, *rest):
    count = len(FLOWS)
    parts, (int_ref, ladder_ref, inter_ref, half, sem) = rest[:count], rest[count:]
    here, core = here_ref[0], here_ref[3]
    pair = (here * CORES + core) * CORES + which
    for f in range(CORES):
        for s in range(dom):
            owner = domain_ref[pair, s] // quarter
            rank = jnp.int32(0)
            for before in range(s):
                rank = rank + (domain_ref[pair, before] // quarter == owner).astype(jnp.int32)
            shift = lax.rem(here - owner + BLOCKS, BLOCKS)
            for flow, (flow_shift, flip) in enumerate(FLOWS):
                if flip == f:

                    @pl.when(shift == flow_shift)
                    def _(flow=flow, rank=rank, f=f, s=s):
                        pltpu.make_async_copy(
                            parts[flow].at[rank], int_ref.at[f, pl.ds(s * TB, TB), :], sem.at[f]
                        ).start()

    rows = 2 * TB
    diagonal = lax.broadcasted_iota(jnp.int32, (rows, rows), 0) == lax.broadcasted_iota(
        jnp.int32, (rows, rows), 1
    )
    for f in range(CORES):
        pltpu.make_async_copy(int_ref.at[f], int_ref.at[f], sem.at[f]).wait()
        total = jnp.zeros((rows, rows), F32)
        for r in range(0, dom * TB, rows):
            acc = lax.dot_general(
                int_ref[f, pl.ds(r, rows), :], amp_ref[which], NT, preferred_element_type=F32
            )
            half[f, pl.ds(r, rows), :] = acc.astype(BF16)
            total = total + acc[:, r : r + rows]
        inter_ref[0, f] = jnp.sum(jnp.where(diagonal, total, 0.0))
    for r in range(0, dom * TB, rows):
        acc = None
        for f in range(CORES):
            term = lax.dot_general(
                int_ref[f, pl.ds(r, rows), :], half[f], NT, preferred_element_type=F32
            )
            acc = term if acc is None else acc + term
        ladder_ref[pl.ds(r, rows), :] = acc


def half_and_ladder(amp, parts, domain, here, which, quarter):
    length = amp.shape[1]
    dom = domain.shape[1]
    vmem = pl.BlockSpec(memory_space=pltpu.VMEM)
    return pl.pallas_call(
        functools.partial(ladder_kernel, quarter, dom, which),
        out_shape=[
            jax.ShapeDtypeStruct((CORES, length, length), BF16),
            jax.ShapeDtypeStruct((length, length), F32),
            jax.ShapeDtypeStruct((1, CORES), F32),
        ],
        grid_spec=pltpu.PrefetchScalarGridSpec(
            num_scalar_prefetch=2,
            grid=(1,),
            in_specs=[vmem] + [pl.BlockSpec(memory_space=pl.ANY)] * len(parts),
            out_specs=[vmem, vmem, pl.BlockSpec(memory_space=pltpu.SMEM)],
            scratch_shapes=[
                pltpu.VMEM((CORES, length, length), BF16),
                pltpu.SemaphoreType.DMA((CORES,)),
            ],
        ),
        compiler_params=pltpu.CompilerParams(vmem_limit_bytes=32 * 2**20),
        cost_estimate=pl.CostEstimate(
            flops=8 * length**3, bytes_accessed=10 * 2**20, transcendentals=0
        ),
        name="half_and_ladder",
    )(domain, here, amp, *parts)


def masked_amps(amps, pair_mask, first_row, dom):
    pairs, rows, length = amps.shape
    row_slot = (first_row + jnp.arange(rows, dtype=jnp.int32)) // TB
    slot_pick = row_slot[:, None] == jnp.arange(dom, dtype=jnp.int32)[None, :]
    row_tiles = jnp.sum(
        jnp.where(slot_pick[None, :, :, None], pair_mask[:, None, :, :], 0), axis=2
    ).astype(BF16)
    tiles = amps.reshape(pairs, rows, dom, TB) * row_tiles[:, :, :, None]
    return tiles.reshape(pairs, rows, length)


def by_core(core, mine, other, axis):
    return jnp.where(
        core == 0,
        jnp.concatenate([mine, other], axis=axis),
        jnp.concatenate([other, mine], axis=axis),
    )


def make_body(ny, nx):
    def body(amps, domain, pair_mask, dfint, coupling):
        pairs, own, length = amps.shape
        dom = domain.shape[1]
        quarter = dfint.shape[1] // TB
        each = pairs // CORES
        z, y, x, c = (lax.axis_index(name).astype(jnp.int32) for name in ("z", "y", "x", "c"))
        here = jnp.stack([z, y, x, c])
        parts = []
        for which in range(each):
            packed = pack(dfint, domain, here, which, quarter)
            parts.append([hop(*flow)(part) for flow, part in zip(FLOWS[:-1], packed)] + [packed[-1]])
        masked = masked_amps(amps, pair_mask, ((y * nx + x) * CORES + c) * own, dom)
        mine = lax.dynamic_slice_in_dim(masked, c * each, each, axis=0)
        other = swap_cores(lax.dynamic_slice_in_dim(masked, (1 - c) * each, each, axis=0))
        amp = lax.all_gather(by_core(c, mine, other, 1), ("y", "x"), axis=1, tiled=True)
        blocks, sums, inters = zip(
            *(half_and_ladder(amp, parts[which], domain, here, which, quarter) for which in range(each))
        )
        inter = jnp.concatenate(inters, axis=0)
        inter = jnp.where(c == 0, inter, inter[:, ::-1])
        spread = jnp.broadcast_to(inter.reshape(1, each * CORES), (BLOCKS * CORES, each * CORES))
        every = lax.all_to_all(spread, ("z", "c"), 0, 0, tiled=True)
        every = every.reshape(BLOCKS * pairs, CORES)
        rows = lax.dynamic_slice_in_dim(coupling, c * each, each, axis=0)
        dressing = jnp.sum(rows[:, :, None] * every[None], axis=1)
        dressing = jnp.where(c == 0, dressing, dressing[:, ::-1])
        chips = ny * nx
        totals = []
        for which in range(each):
            total = sums[which]
            for f in range(CORES):
                total = total + dressing[which, f] * blocks[which][f].astype(F32)
            totals.append(total.astype(BF16).reshape(chips, 1, length // chips, length))
        sent = jnp.concatenate(totals, axis=1)
        got = lax.all_to_all(sent, ("y", "x"), 0, 0, tiled=True)
        result = jnp.sum(got.astype(F32), axis=0).astype(BF16)
        mine = lax.dynamic_slice_in_dim(result, c * own, own, axis=1)
        other = swap_cores(lax.dynamic_slice_in_dim(result, (1 - c) * own, own, axis=1))
        return by_core(c, mine, other, 0)

    return body


def solution(mesh):
    ny = nx = 4
    grid = Mesh(mesh.devices.reshape(BLOCKS, ny, nx, CORES), ("z", "y", "x", "c"))
    virt = ("y", "x", "c")
    return jax.shard_map(
        make_body(ny, nx),
        mesh=grid,
        in_specs=(P("z", virt, None), P(), P("z", None, None), P(virt, "z", None), P("z", None)),
        out_specs=P("z", virt, None),
        check_vma=False,
    )
```

```python
import functools

import jax
import jax.numpy as jnp
from jax import lax
from jax.experimental import pallas as pl
from jax.experimental.pallas import tpu as pltpu
from jax.sharding import Mesh
from jax.sharding import PartitionSpec as P

TB = 128
BLOCKS = 4
CORES = 2
SLOTS = 2
VMEM_LIMIT = 56 * 2**20
BF16 = jnp.bfloat16
F32 = jnp.float32
NT = (((1,), (1,)), ((), ()))
SHIFTS = (1, 3, 2, 0)


def hop(shift, flip):
    perm = [
        (z * CORES + c, (z + shift) % BLOCKS * CORES + (c ^ flip))
        for z in range(BLOCKS)
        for c in range(CORES)
    ]
    return functools.partial(lax.ppermute, axis_name=("z", "c"), perm=perm)


def swap_cores(value):
    return lax.ppermute(value, "c", [(0, 1), (1, 0)])


def block_slots(domain_ref, pair, block, quarter, dom):
    found = jnp.int32(0)
    first = jnp.int32(0)
    second = jnp.int32(0)
    for s in range(dom):
        inside = domain_ref[pair, s] // quarter == block
        first = jnp.where(inside & (found == 0), s, first)
        second = jnp.where(inside & (found == 1), s, second)
        found = found + inside.astype(jnp.int32)
    return first, second


def pack_kernel(quarter, dom, which, flip, domain_ref, here_ref, dfint_ref, *rest):
    count = len(SHIFTS)
    outs, (buffer, in_sem, out_sem) = rest[:count], rest[count:]
    here, core = here_ref[0], here_ref[3]
    for n, shift in enumerate(SHIFTS):
        target = lax.rem(here + shift, BLOCKS)
        pair = (target * CORES + (core ^ flip)) * CORES + which
        for j, slot in enumerate(block_slots(domain_ref, pair, here, quarter, dom)):
            row = jnp.clip(domain_ref[pair, slot] - here * quarter, 0, quarter - 1)
            for t in range(dom):
                column = domain_ref[pair, t]
                pltpu.make_async_copy(
                    dfint_ref.at[
                        0,
                        pl.ds(pl.multiple_of(row * TB, TB), TB),
                        pl.ds(pl.multiple_of(column * TB, TB), TB),
                    ],
                    buffer.at[n, j, :, pl.ds(t * TB, TB)],
                    in_sem.at[n],
                ).start()
    for n in range(count):
        pltpu.make_async_copy(buffer.at[n], buffer.at[n], in_sem.at[n]).wait()
        pltpu.make_async_copy(buffer.at[n], outs[n], out_sem.at[n]).start()
    for n in range(count):
        pltpu.make_async_copy(buffer.at[n], outs[n], out_sem.at[n]).wait()


def pack(dfint, domain, here, which, flip, quarter):
    dom = domain.shape[1]
    count = len(SHIFTS)
    tile_rows = (SLOTS, TB, dom * TB)
    return pl.pallas_call(
        functools.partial(pack_kernel, quarter, dom, which, flip),
        out_shape=[jax.ShapeDtypeStruct(tile_rows, BF16)] * count,
        grid_spec=pltpu.PrefetchScalarGridSpec(
            num_scalar_prefetch=2,
            grid=(1,),
            in_specs=[pl.BlockSpec(memory_space=pl.ANY)],
            out_specs=[pl.BlockSpec(memory_space=pl.ANY)] * count,
            scratch_shapes=[
                pltpu.VMEM((count,) + tile_rows, BF16),
                pltpu.SemaphoreType.DMA((count,)),
                pltpu.SemaphoreType.DMA((count,)),
            ],
        ),
        compiler_params=pltpu.CompilerParams(vmem_limit_bytes=VMEM_LIMIT),
        cost_estimate=pl.CostEstimate(flops=0, bytes_accessed=7 * 2**20, transcendentals=0),
        name="pack_tiles",
    )(domain, here, dfint)


def half_kernel(quarter, dom, which, flip, domain_ref, here_ref, amp_ref, before_ref, *rest):
    count = len(SHIFTS)
    parts, (int_ref, half_ref, inter_ref, sem) = rest[:count], rest[count:]
    here, core = here_ref[0], here_ref[3]
    pair = (here * CORES + core) * CORES + which
    for s in range(dom):
        owner = domain_ref[pair, s] // quarter
        rank = jnp.int32(0)
        for earlier in range(s):
            rank = rank + (domain_ref[pair, earlier] // quarter == owner).astype(jnp.int32)
        shift = lax.rem(here - owner + BLOCKS, BLOCKS)
        for n, flow_shift in enumerate(SHIFTS):

            @pl.when(shift == flow_shift)
            def _(n=n, rank=rank, s=s):
                pltpu.make_async_copy(
                    parts[n].at[rank], int_ref.at[pl.ds(s * TB, TB), :], sem.at[0]
                ).start()

    rows = 2 * TB
    pltpu.make_async_copy(int_ref, int_ref, sem.at[0]).wait()
    total = jnp.zeros((rows, rows), F32)
    for r in range(0, dom * TB, rows):
        acc = lax.dot_general(
            int_ref[pl.ds(r, rows), :], amp_ref[...], NT, preferred_element_type=F32
        )
        half_ref[pl.ds(r, rows), :] = acc.astype(BF16)
        total = total + acc[:, r : r + rows]
    diagonal = lax.broadcasted_iota(jnp.int32, (rows, rows), 0) == lax.broadcasted_iota(
        jnp.int32, (rows, rows), 1
    )
    trace = jnp.sum(jnp.where(diagonal, total, 0.0))
    lane = lax.broadcasted_iota(jnp.int32, inter_ref.shape, 1)
    inter_ref[...] = jnp.where(lane == which * CORES + flip, trace, before_ref[...])


def half_ladder(amp, before, parts, domain, here, which, flip, quarter):
    length = amp.shape[0]
    vmem = pl.BlockSpec(memory_space=pltpu.VMEM)
    square = jax.ShapeDtypeStruct((length, length), BF16)
    return pl.pallas_call(
        functools.partial(half_kernel, quarter, domain.shape[1], which, flip),
        out_shape=[square, square, jax.ShapeDtypeStruct(before.shape, F32)],
        grid_spec=pltpu.PrefetchScalarGridSpec(
            num_scalar_prefetch=2,
            grid=(1,),
            in_specs=[vmem, vmem] + [pl.BlockSpec(memory_space=pl.ANY)] * len(parts),
            out_specs=[vmem] * 3,
            scratch_shapes=[pltpu.SemaphoreType.DMA((1,))],
        ),
        compiler_params=pltpu.CompilerParams(vmem_limit_bytes=VMEM_LIMIT),
        cost_estimate=pl.CostEstimate(
            flops=2 * length**3, bytes_accessed=10 * length**2, transcendentals=0
        ),
        name="half_ladder",
    )(domain, here, amp, before, *parts)


def ladder_kernel(int_ref, half_ref, *rest):
    out_ref = rest[-1]
    acc = lax.dot_general(int_ref[...], half_ref[...], NT, preferred_element_type=F32)
    out_ref[...] = acc if len(rest) == 1 else acc + rest[0][...]


def ladder(ints, half, *before):
    length = half.shape[0]
    rows = length // 3
    block = pl.BlockSpec((rows, length), lambda i: (i, 0))
    return pl.pallas_call(
        ladder_kernel,
        out_shape=jax.ShapeDtypeStruct((length, length), F32),
        grid=(length // rows,),
        in_specs=[block, pl.BlockSpec((length, length), lambda i: (0, 0))] + [block] * len(before),
        out_specs=block,
        compiler_params=pltpu.CompilerParams(vmem_limit_bytes=VMEM_LIMIT),
        cost_estimate=pl.CostEstimate(
            flops=2 * length**3, bytes_accessed=12 * length**2, transcendentals=0
        ),
        name="ladder",
    )(ints, half, *before)


def cycle_kernel(which, ny, nx, here_ref, coupling_ref, inter_ref, *rest):
    ints, ladder_ref, outs = rest[:CORES], rest[CORES], rest[CORES + 1 :]
    y, x, core = here_ref[1], here_ref[2], here_ref[3]
    step = pl.program_id(0)
    dressing = []
    for f in range(CORES):
        total = jnp.float32(0)
        for source in range(BLOCKS * CORES):
            flip = (source % CORES) ^ core ^ f
            for w in range(CORES):
                total = total + coupling_ref[core * CORES + which, source * CORES + w] * (
                    inter_ref[source, w * CORES + flip]
                )
        dressing.append(total)
    rows = outs[0].shape[1]

    def chip_rows(xx):
        spot = pl.ds(pl.multiple_of(xx * rows, rows), rows)
        total = ladder_ref[spot, :]
        for f in range(CORES):
            total = total + dressing[f] * ints[f][spot, :].astype(F32)
        return total

    if which == 0:
        for s in range(nx):
            outs[s][0] = chip_rows(lax.rem(x + s, nx)).astype(outs[s].dtype)
    else:
        for s in range(ny):

            @pl.when(step == s)
            def _(s=s):
                for k in range(nx):
                    outs[s][k] = chip_rows(lax.rem(x + k, nx)).astype(outs[s].dtype)


def add_cycle(ladder_sum, ints, inter, coupling, here, which, ny, nx):
    length = ladder_sum.shape[0]
    rows = length // (ny * nx)
    smem = pl.BlockSpec(memory_space=pltpu.SMEM)
    block = pl.BlockSpec((nx * rows, length), lambda t, where: (lax.rem(where[1] + t, ny), 0))
    if which == 0:
        count, shape = nx, (ny, rows, length)
        out = pl.BlockSpec((1, rows, length), lambda t, where: (t, 0, 0))
    else:
        count, shape = ny, (nx, rows, length)
        out = pl.BlockSpec(shape, lambda t, where: (0, 0, 0))
    return pl.pallas_call(
        functools.partial(cycle_kernel, which, ny, nx),
        out_shape=[jax.ShapeDtypeStruct(shape, BF16 if s else F32) for s in range(count)],
        grid_spec=pltpu.PrefetchScalarGridSpec(
            num_scalar_prefetch=1,
            grid=(ny,),
            in_specs=[smem, smem] + [block] * (CORES + 1),
            out_specs=[out] * count,
        ),
        compiler_params=pltpu.CompilerParams(vmem_limit_bytes=VMEM_LIMIT),
        cost_estimate=pl.CostEstimate(
            flops=6 * length**2, bytes_accessed=12 * length**2, transcendentals=0
        ),
        name="add_cycle",
    )(here, coupling, inter, *ints, ladder_sum)


def sum_over(axis, size, parts):
    total = parts[0].astype(F32)
    for s in (1, 3, 2):
        perm = [(i, (i + s) % size) for i in range(size)]
        total = total + lax.ppermute(parts[s].astype(BF16), axis, perm).astype(F32)
    return total


def masked_amps(amps, pair_mask, first_row, dom):
    pairs, rows, length = amps.shape
    row_slot = (first_row + jnp.arange(rows, dtype=jnp.int32)) // TB
    slot_pick = row_slot[:, None] == jnp.arange(dom, dtype=jnp.int32)[None, :]
    row_tiles = jnp.sum(
        jnp.where(slot_pick[None, :, :, None], pair_mask[:, None, :, :], 0), axis=2
    ).astype(BF16)
    tiles = amps.reshape(pairs, rows, dom, TB) * row_tiles[:, :, :, None]
    return tiles.reshape(pairs, rows, length)


def by_core(core, mine, other, axis):
    return jnp.where(
        core == 0,
        jnp.concatenate([mine, other], axis=axis),
        jnp.concatenate([other, mine], axis=axis),
    )


def make_body(ny, nx):
    def gather(rows, chips):
        return lax.all_to_all(
            jnp.broadcast_to(rows[None], (chips,) + rows.shape), ("y", "x"), 0, 0, tiled=True
        ).reshape(chips * rows.shape[0], rows.shape[1])

    def body(amps, domain, pair_mask, dfint, coupling):
        pairs, own, length = amps.shape
        dom = domain.shape[1]
        quarter = dfint.shape[1] // TB
        each = pairs // CORES
        chips = ny * nx
        z, y, x, c = (lax.axis_index(name).astype(jnp.int32) for name in ("z", "y", "x", "c"))
        here = jnp.stack([z, y, x, c])
        order = [(which, f) for which in range(each) for f in range(CORES)]
        packed = {key: pack(dfint, domain, here, *key, quarter) for key in order[:1]}
        packed[order[0]], amps = lax.optimization_barrier((packed[order[0]], amps))
        for key in order[1:]:
            packed[key] = pack(dfint, domain, here, *key, quarter)
        parts = {
            (which, f): [
                part if (s, f) == (0, 0) else hop(s, f)(part)
                for s, part in zip(SHIFTS, packed[which, f])
            ]
            for which, f in order
        }
        masked = masked_amps(amps, pair_mask, ((y * nx + x) * CORES + c) * own, dom)
        mine = lax.dynamic_slice_in_dim(masked, c * each, each, axis=0)
        other = swap_cores(lax.dynamic_slice_in_dim(masked, (1 - c) * each, each, axis=0))
        both = by_core(c, mine, other, 1)
        inter = jnp.zeros((BLOCKS * CORES, TB), F32)
        sums, blocks = [None] * each, [[] for _ in range(each)]
        for which in range(each):
            amp = gather(both[which], chips)
            for f in range(CORES):
                ints, half, inter = half_ladder(
                    amp, inter, parts[which, f], domain, here, which, f, quarter
                )
                blocks[which].append(ints)
                sums[which] = ladder(ints, half, *([] if f == 0 else [sums[which]]))
        every = lax.all_to_all(inter, ("z", "c"), 0, 0, tiled=True)
        ends = []
        for which in range(each):
            (first, n1), (second, n2) = (("x", nx), ("y", ny))[:: 1 if which == 0 else -1]
            parts_out = add_cycle(
                sums[which], blocks[which], every, coupling, here, which, ny, nx
            )
            stage = sum_over(first, n1, parts_out)
            ends.append(sum_over(second, n2, [stage[s] for s in range(n2)]))
        result = jnp.stack(ends).astype(BF16)
        mine = lax.dynamic_slice_in_dim(result, c * own, own, axis=1)
        other = swap_cores(lax.dynamic_slice_in_dim(result, (1 - c) * own, own, axis=1))
        return by_core(c, mine, other, 0)

    return body


def solution(mesh):
    ny = nx = 4
    grid = Mesh(mesh.devices.reshape(BLOCKS, ny, nx, CORES), ("z", "y", "x", "c"))
    virt = ("y", "x", "c")
    return jax.shard_map(
        make_body(ny, nx),
        mesh=grid,
        in_specs=(P("z", virt, None), P(), P("z", None, None), P(virt, "z", None), P("z", None)),
        out_specs=P("z", virt, None),
        check_vma=False,
    )
```

```python
import functools

import jax
import jax.numpy as jnp
from jax import lax
from jax.experimental import pallas as pl
from jax.experimental.pallas import tpu as pltpu
from jax.sharding import Mesh
from jax.sharding import PartitionSpec as P

TB = 128
BLOCKS = 4
CORES = 2
SLOTS = 2
VMEM_LIMIT = 56 * 2**20
BF16 = jnp.bfloat16
F32 = jnp.float32
NT = (((1,), (1,)), ((), ()))
SHIFTS = (1, 3, 2, 0)


def hop(shift, flip):
    perm = [
        (z * CORES + c, (z + shift) % BLOCKS * CORES + (c ^ flip))
        for z in range(BLOCKS)
        for c in range(CORES)
    ]
    return functools.partial(lax.ppermute, axis_name=("z", "c"), perm=perm)


def swap_cores(value):
    return lax.ppermute(value, "c", [(0, 1), (1, 0)])


def block_slots(domain_ref, pair, block, quarter, dom):
    found = jnp.int32(0)
    first = jnp.int32(0)
    second = jnp.int32(0)
    for s in range(dom):
        inside = domain_ref[pair, s] // quarter == block
        first = jnp.where(inside & (found == 0), s, first)
        second = jnp.where(inside & (found == 1), s, second)
        found = found + inside.astype(jnp.int32)
    return first, second


def pack_kernel(quarter, dom, which, flip, domain_ref, here_ref, dfint_ref, *rest):
    count = len(SHIFTS)
    outs, (buffer, in_sem, out_sem) = rest[:count], rest[count:]
    here, core = here_ref[0], here_ref[3]
    for n, shift in enumerate(SHIFTS):
        target = lax.rem(here + shift, BLOCKS)
        pair = (target * CORES + (core ^ flip)) * CORES + which
        for j, slot in enumerate(block_slots(domain_ref, pair, here, quarter, dom)):
            row = jnp.clip(domain_ref[pair, slot] - here * quarter, 0, quarter - 1)
            for t in range(dom):
                column = domain_ref[pair, t]
                pltpu.make_async_copy(
                    dfint_ref.at[
                        0,
                        pl.ds(pl.multiple_of(row * TB, TB), TB),
                        pl.ds(pl.multiple_of(column * TB, TB), TB),
                    ],
                    buffer.at[n, j, :, pl.ds(t * TB, TB)],
                    in_sem.at[n],
                ).start()
    for n in range(count):
        pltpu.make_async_copy(buffer.at[n], buffer.at[n], in_sem.at[n]).wait()
        pltpu.make_async_copy(buffer.at[n], outs[n], out_sem.at[n]).start()
    for n in range(count):
        pltpu.make_async_copy(buffer.at[n], outs[n], out_sem.at[n]).wait()


def pack(dfint, domain, here, which, flip, quarter):
    dom = domain.shape[1]
    count = len(SHIFTS)
    tile_rows = (SLOTS, TB, dom * TB)
    return pl.pallas_call(
        functools.partial(pack_kernel, quarter, dom, which, flip),
        out_shape=[jax.ShapeDtypeStruct(tile_rows, BF16)] * count,
        grid_spec=pltpu.PrefetchScalarGridSpec(
            num_scalar_prefetch=2,
            grid=(1,),
            in_specs=[pl.BlockSpec(memory_space=pl.ANY)],
            out_specs=[pl.BlockSpec(memory_space=pl.ANY)] * count,
            scratch_shapes=[
                pltpu.VMEM((count,) + tile_rows, BF16),
                pltpu.SemaphoreType.DMA((count,)),
                pltpu.SemaphoreType.DMA((count,)),
            ],
        ),
        compiler_params=pltpu.CompilerParams(vmem_limit_bytes=VMEM_LIMIT),
        cost_estimate=pl.CostEstimate(flops=0, bytes_accessed=7 * 2**20, transcendentals=0),
        name="pack_tiles",
    )(domain, here, dfint)


def work_kernel(quarter, dom, which, flips, finish, domain_ref, here_ref, amp_ref, before_ref, *rest):
    count = len(SHIFTS)
    parts, rest = rest[: count * len(flips)], rest[count * len(flips) :]
    int_out, out_ref, inter_ref, amp, ints, half, ladder, in_sem, out_sem = rest
    here, core = here_ref[0], here_ref[3]
    pair = (here * CORES + core) * CORES + which
    load_amp = pltpu.make_async_copy(amp_ref, amp, in_sem.at[len(flips)])
    load_amp.start()
    for s in range(dom):
        owner = domain_ref[pair, s] // quarter
        rank = jnp.int32(0)
        for earlier in range(s):
            rank = rank + (domain_ref[pair, earlier] // quarter == owner).astype(jnp.int32)
        shift = lax.rem(here - owner + BLOCKS, BLOCKS)
        for n, flow_shift in enumerate(SHIFTS):

            @pl.when(shift == flow_shift)
            def _(n=n, rank=rank, s=s):
                for f in range(len(flips)):
                    pltpu.make_async_copy(
                        parts[f * count + n].at[rank],
                        ints.at[f, pl.ds(s * TB, TB), :],
                        in_sem.at[f],
                    ).start()

    load_amp.wait()
    rows = 2 * TB
    diagonal = lax.broadcasted_iota(jnp.int32, (rows, rows), 0) == lax.broadcasted_iota(
        jnp.int32, (rows, rows), 1
    )
    lane = lax.broadcasted_iota(jnp.int32, inter_ref.shape, 1)
    inter = before_ref[...]
    for f, flip in enumerate(flips):
        pltpu.make_async_copy(ints.at[f], ints.at[f], in_sem.at[f]).wait()
        pltpu.make_async_copy(ints.at[f], int_out.at[f], out_sem.at[f]).start()
        total = jnp.zeros((rows, rows), F32)
        for r in range(0, dom * TB, rows):
            spot = pl.ds(r, rows)
            acc = lax.dot_general(ints[f, spot, :], amp[...], NT, preferred_element_type=F32)
            half[f, spot, :] = acc.astype(BF16)
            total = total + acc[:, r : r + rows]
            if not finish:
                pltpu.make_async_copy(
                    half.at[f, spot, :], out_ref.at[f, spot, :], out_sem.at[len(flips)]
                ).start()
        trace = jnp.sum(jnp.where(diagonal, total, 0.0))
        inter = jnp.where(lane == which * CORES + flip, trace, inter)
    inter_ref[...] = inter
    if finish:
        for r in range(0, dom * TB, rows):
            spot = pl.ds(r, rows)
            acc = None
            for f in range(len(flips)):
                term = lax.dot_general(ints[f, spot, :], half[f], NT, preferred_element_type=F32)
                acc = term if acc is None else acc + term
            ladder[spot, :] = acc
            pltpu.make_async_copy(
                ladder.at[spot, :], out_ref.at[spot, :], out_sem.at[len(flips)]
            ).start()
    for f in range(len(flips)):
        pltpu.make_async_copy(ints.at[f], int_out.at[f], out_sem.at[f]).wait()
    pltpu.make_async_copy(ladder if finish else half, out_ref, out_sem.at[len(flips)]).wait()


def work(amp, before, parts, domain, here, which, flips, finish, quarter):
    length = amp.shape[0]
    count = len(flips)
    small = pl.BlockSpec(memory_space=pltpu.VMEM)
    anywhere = pl.BlockSpec(memory_space=pl.ANY)
    squares = (count, length, length)
    return pl.pallas_call(
        functools.partial(work_kernel, quarter, domain.shape[1], which, flips, finish),
        out_shape=[
            jax.ShapeDtypeStruct(squares, BF16),
            jax.ShapeDtypeStruct((length, length), F32)
            if finish
            else jax.ShapeDtypeStruct(squares, BF16),
            jax.ShapeDtypeStruct(before.shape, F32),
        ],
        grid_spec=pltpu.PrefetchScalarGridSpec(
            num_scalar_prefetch=2,
            grid=(1,),
            in_specs=[anywhere, small] + [anywhere] * len(parts),
            out_specs=[anywhere, anywhere, small],
            scratch_shapes=[
                pltpu.VMEM((length, length), BF16),
                pltpu.VMEM(squares, BF16),
                pltpu.VMEM(squares, BF16),
                pltpu.VMEM((length, length), F32),
                pltpu.SemaphoreType.DMA((count + 1,)),
                pltpu.SemaphoreType.DMA((count + 1,)),
            ],
        ),
        compiler_params=pltpu.CompilerParams(vmem_limit_bytes=VMEM_LIMIT),
        cost_estimate=pl.CostEstimate(
            flops=(4 if finish else 2) * count * length**3,
            bytes_accessed=10 * count * length**2,
            transcendentals=0,
        ),
        name="half_and_ladder" if finish else "half_ladder",
    )(domain, here, amp, before, *parts)


def ladder_kernel(int_ref, half_ref, *rest):
    out_ref = rest[-1]
    acc = lax.dot_general(int_ref[0], half_ref[0], NT, preferred_element_type=F32)
    out_ref[...] = acc + rest[0][...]


def ladder(ints, half, before):
    length = before.shape[0]
    rows = length // 3
    block = pl.BlockSpec((rows, length), lambda i: (i, 0))
    int_block = pl.BlockSpec((1, rows, length), lambda i: (0, i, 0))
    return pl.pallas_call(
        ladder_kernel,
        out_shape=jax.ShapeDtypeStruct((length, length), F32),
        grid=(length // rows,),
        in_specs=[int_block, pl.BlockSpec((1, length, length), lambda i: (0, 0, 0)), block],
        out_specs=block,
        compiler_params=pltpu.CompilerParams(vmem_limit_bytes=VMEM_LIMIT),
        cost_estimate=pl.CostEstimate(
            flops=2 * length**3, bytes_accessed=12 * length**2, transcendentals=0
        ),
        name="ladder",
    )(ints, half, before)


def cycle_kernel(which, ny, nx, here_ref, coupling_ref, inter_ref, *rest):
    ints, ladder_ref, outs, dressing = rest[:CORES], rest[CORES], rest[CORES + 1 : -1], rest[-1]
    y, x, core = here_ref[1], here_ref[2], here_ref[3]
    step = pl.program_id(0)

    @pl.when(step == 0)
    def _():
        for f in range(CORES):
            total = jnp.float32(0)
            for source in range(BLOCKS * CORES):
                flip = (source % CORES) ^ core ^ f
                for w in range(CORES):
                    total = total + coupling_ref[core * CORES + which, source * CORES + w] * (
                        inter_ref[source, w * CORES + flip]
                    )
            dressing[f] = total

    rows = outs[0].shape[1]

    def chip_rows(xx):
        spot = pl.ds(pl.multiple_of(xx * rows, rows), rows)
        total = ladder_ref[spot, :]
        for f in range(CORES):
            total = total + dressing[f] * ints[f][0, spot, :].astype(F32)
        return total

    if which == 0:
        for s in range(nx):
            outs[s][0] = chip_rows(lax.rem(x + s, nx)).astype(outs[s].dtype)
    else:
        for s in range(ny):

            @pl.when(step == s)
            def _(s=s):
                for k in range(nx):
                    outs[s][k] = chip_rows(lax.rem(x + k, nx)).astype(outs[s].dtype)


def add_cycle(ladder_sum, ints, inter, coupling, here, which, ny, nx):
    length = ladder_sum.shape[0]
    rows = length // (ny * nx)
    smem = pl.BlockSpec(memory_space=pltpu.SMEM)
    block = pl.BlockSpec((nx * rows, length), lambda t, where: (lax.rem(where[1] + t, ny), 0))
    int_blocks = [
        pl.BlockSpec(
            (1, nx * rows, length), lambda t, where, n=n: (n, lax.rem(where[1] + t, ny), 0)
        )
        for _, n in ints
    ]
    if which == 0:
        count, shape = nx, (ny, rows, length)
        out = pl.BlockSpec((1, rows, length), lambda t, where: (t, 0, 0))
    else:
        count, shape = ny, (nx, rows, length)
        out = pl.BlockSpec(shape, lambda t, where: (0, 0, 0))
    return pl.pallas_call(
        functools.partial(cycle_kernel, which, ny, nx),
        out_shape=[jax.ShapeDtypeStruct(shape, BF16 if s else F32) for s in range(count)],
        grid_spec=pltpu.PrefetchScalarGridSpec(
            num_scalar_prefetch=1,
            grid=(ny,),
            in_specs=[smem, smem] + int_blocks + [block],
            out_specs=[out] * count,
            scratch_shapes=[pltpu.SMEM((CORES,), F32)],
        ),
        compiler_params=pltpu.CompilerParams(vmem_limit_bytes=VMEM_LIMIT),
        cost_estimate=pl.CostEstimate(
            flops=6 * length**2, bytes_accessed=12 * length**2, transcendentals=0
        ),
        name="add_cycle",
    )(here, coupling, inter, *(array for array, _ in ints), ladder_sum)


def sum_over(axis, size, parts):
    total = parts[0].astype(F32)
    for s in (1, 3, 2):
        perm = [(i, (i + s) % size) for i in range(size)]
        total = total + lax.ppermute(parts[s].astype(BF16), axis, perm).astype(F32)
    return total


def masked_amps(amps, pair_mask, first_row, dom):
    pairs, rows, length = amps.shape
    row_slot = (first_row + jnp.arange(rows, dtype=jnp.int32)) // TB
    slot_pick = row_slot[:, None] == jnp.arange(dom, dtype=jnp.int32)[None, :]
    row_tiles = jnp.sum(
        jnp.where(slot_pick[None, :, :, None], pair_mask[:, None, :, :], 0), axis=2
    ).astype(BF16)
    tiles = amps.reshape(pairs, rows, dom, TB) * row_tiles[:, :, :, None]
    return tiles.reshape(pairs, rows, length)


def by_core(core, mine, other, axis):
    return jnp.where(
        core == 0,
        jnp.concatenate([mine, other], axis=axis),
        jnp.concatenate([other, mine], axis=axis),
    )


def make_body(ny, nx):
    def gather(rows, chips):
        return lax.all_to_all(
            jnp.broadcast_to(rows[None], (chips,) + rows.shape), ("y", "x"), 0, 0, tiled=True
        ).reshape(chips * rows.shape[0], rows.shape[1])

    def body(amps, domain, pair_mask, dfint, coupling):
        pairs, own, length = amps.shape
        dom = domain.shape[1]
        quarter = dfint.shape[1] // TB
        each = pairs // CORES
        chips = ny * nx
        z, y, x, c = (lax.axis_index(name).astype(jnp.int32) for name in ("z", "y", "x", "c"))
        here = jnp.stack([z, y, x, c])
        order = [(which, f) for which in range(each) for f in range(CORES)]
        parts = {}
        for which, f in order:
            packed = pack(dfint, domain, here, which, f, quarter)
            if not parts:
                packed, amps = lax.optimization_barrier((packed, amps))
            parts[which, f] = [
                part if (s, f) == (0, 0) else hop(s, f)(part) for s, part in zip(SHIFTS, packed)
            ]
        masked = masked_amps(amps, pair_mask, ((y * nx + x) * CORES + c) * own, dom)
        mine = lax.dynamic_slice_in_dim(masked, c * each, each, axis=0)
        other = swap_cores(lax.dynamic_slice_in_dim(masked, (1 - c) * each, each, axis=0))
        parts[order[0]], both = lax.optimization_barrier(
            (parts[order[0]], by_core(c, mine, other, 1))
        )
        amp = [gather(both[0], chips), None]
        amp[0], later = lax.optimization_barrier((amp[0], both[1]))
        amp[1] = gather(later, chips)
        inter = jnp.zeros((BLOCKS * CORES, TB), F32)
        ints0, ladder0, inter = work(
            amp[0], inter, parts[0, 0] + parts[0, 1], domain, here, 0, (0, 1), True, quarter
        )
        ints1, ladder1, inter = work(
            amp[1], inter, parts[1, 0], domain, here, 1, (0,), True, quarter
        )
        ints2, half, inter = work(
            amp[1], inter, parts[1, 1], domain, here, 1, (1,), False, quarter
        )
        sums = [ladder0, ladder(ints2, half, ladder1)]
        blocks = [[(ints0, 0), (ints0, 1)], [(ints1, 0), (ints2, 0)]]
        every = lax.all_to_all(inter, ("z", "c"), 0, 0, tiled=True)
        ends = []
        for which in range(each):
            (first, n1), (second, n2) = (("x", nx), ("y", ny))[:: 1 if which == 0 else -1]
            parts_out = add_cycle(
                sums[which], blocks[which], every, coupling, here, which, ny, nx
            )
            stage = sum_over(first, n1, parts_out)
            ends.append(sum_over(second, n2, [stage[s] for s in range(n2)]))
        result = jnp.stack(ends).astype(BF16)
        mine = lax.dynamic_slice_in_dim(result, c * own, own, axis=1)
        other = swap_cores(lax.dynamic_slice_in_dim(result, (1 - c) * own, own, axis=1))
        return by_core(c, mine, other, 0)

    return body


def solution(mesh):
    ny = nx = 4
    grid = Mesh(mesh.devices.reshape(BLOCKS, ny, nx, CORES), ("z", "y", "x", "c"))
    virt = ("y", "x", "c")
    return jax.shard_map(
        make_body(ny, nx),
        mesh=grid,
        in_specs=(P("z", virt, None), P(), P("z", None, None), P(virt, "z", None), P("z", None)),
        out_specs=P("z", virt, None),
        check_vma=False,
    )
```

```python
import functools

import jax
import jax.numpy as jnp
from jax import lax
from jax.experimental import pallas as pl
from jax.experimental.pallas import tpu as pltpu
from jax.sharding import Mesh
from jax.sharding import PartitionSpec as P

TB = 128
BLOCKS = 4
CORES = 2
SLOTS = 2
VMEM_LIMIT = 56 * 2**20
BF16 = jnp.bfloat16
F32 = jnp.float32
NT = (((1,), (1,)), ((), ()))
SHIFTS = (1, 3, 2, 0)
EARLY = 1
FIRST = (((0, 0), 0), ((0, 0), 1), ((0, 0), 2))


def hop(shift, flip):
    perm = [
        (z * CORES + c, (z + shift) % BLOCKS * CORES + (c ^ flip))
        for z in range(BLOCKS)
        for c in range(CORES)
    ]
    return functools.partial(lax.ppermute, axis_name=("z", "c"), perm=perm)


def swap_cores(value):
    return lax.ppermute(value, "c", [(0, 1), (1, 0)])


def block_slots(domain_ref, pair, block, quarter, dom):
    found = jnp.int32(0)
    first = jnp.int32(0)
    second = jnp.int32(0)
    for s in range(dom):
        inside = domain_ref[pair, s] // quarter == block
        first = jnp.where(inside & (found == 0), s, first)
        second = jnp.where(inside & (found == 1), s, second)
        found = found + inside.astype(jnp.int32)
    return first, second


def pack_kernel(quarter, dom, which, flip, domain_ref, here_ref, dfint_ref, *rest):
    count = len(SHIFTS)
    outs, (buffer, in_sem, out_sem) = rest[:count], rest[count:]
    here, core = here_ref[0], here_ref[3]
    for n, shift in enumerate(SHIFTS):
        target = lax.rem(here + shift, BLOCKS)
        pair = (target * CORES + (core ^ flip)) * CORES + which
        for j, slot in enumerate(block_slots(domain_ref, pair, here, quarter, dom)):
            row = jnp.clip(domain_ref[pair, slot] - here * quarter, 0, quarter - 1)
            for t in range(dom):
                column = domain_ref[pair, t]
                pltpu.make_async_copy(
                    dfint_ref.at[
                        0,
                        pl.ds(pl.multiple_of(row * TB, TB), TB),
                        pl.ds(pl.multiple_of(column * TB, TB), TB),
                    ],
                    buffer.at[n, j, :, pl.ds(t * TB, TB)],
                    in_sem.at[n],
                ).start()
    for n in range(count):
        pltpu.make_async_copy(buffer.at[n], buffer.at[n], in_sem.at[n]).wait()
        pltpu.make_async_copy(buffer.at[n], outs[n], out_sem.at[n]).start()
    for n in range(count):
        pltpu.make_async_copy(buffer.at[n], outs[n], out_sem.at[n]).wait()


def pack(dfint, domain, here, which, flip, quarter):
    dom = domain.shape[1]
    count = len(SHIFTS)
    tile_rows = (SLOTS, TB, dom * TB)
    return pl.pallas_call(
        functools.partial(pack_kernel, quarter, dom, which, flip),
        out_shape=[jax.ShapeDtypeStruct(tile_rows, BF16)] * count,
        grid_spec=pltpu.PrefetchScalarGridSpec(
            num_scalar_prefetch=2,
            grid=(1,),
            in_specs=[pl.BlockSpec(memory_space=pl.ANY)],
            out_specs=[pl.BlockSpec(memory_space=pl.ANY)] * count,
            scratch_shapes=[
                pltpu.VMEM((count,) + tile_rows, BF16),
                pltpu.SemaphoreType.DMA((count,)),
                pltpu.SemaphoreType.DMA((count,)),
            ],
        ),
        compiler_params=pltpu.CompilerParams(vmem_limit_bytes=VMEM_LIMIT),
        cost_estimate=pl.CostEstimate(flops=0, bytes_accessed=7 * 2**20, transcendentals=0),
        name="pack_tiles",
    )(domain, here, dfint)


def work_kernel(quarter, dom, which, flips, finish, domain_ref, here_ref, amp_ref, before_ref, *rest):
    count = len(SHIFTS)
    parts, rest = rest[: count * len(flips)], rest[count * len(flips) :]
    int_out, out_ref, inter_out, amp, ints, half, ladder, inter_ref, in_sem, out_sem = rest
    here, core = here_ref[0], here_ref[3]
    pair = (here * CORES + core) * CORES + which
    load_amp = pltpu.make_async_copy(amp_ref, amp, in_sem.at[len(flips)])
    load_amp.start()
    load_inter = pltpu.make_async_copy(before_ref, inter_ref, in_sem.at[len(flips) + 1])
    load_inter.start()
    for s in range(dom):
        owner = domain_ref[pair, s] // quarter
        rank = jnp.int32(0)
        for earlier in range(s):
            rank = rank + (domain_ref[pair, earlier] // quarter == owner).astype(jnp.int32)
        shift = lax.rem(here - owner + BLOCKS, BLOCKS)
        for n, flow_shift in enumerate(SHIFTS):

            @pl.when(shift == flow_shift)
            def _(n=n, rank=rank, s=s):
                for f in range(len(flips)):
                    pltpu.make_async_copy(
                        parts[f * count + n].at[rank],
                        ints.at[f, pl.ds(s * TB, TB), :],
                        in_sem.at[f],
                    ).start()

    load_amp.wait()
    rows = 2 * TB
    diagonal = lax.broadcasted_iota(jnp.int32, (rows, rows), 0) == lax.broadcasted_iota(
        jnp.int32, (rows, rows), 1
    )
    lane = lax.broadcasted_iota(jnp.int32, inter_ref.shape, 1)
    traces = []
    for f, flip in enumerate(flips):
        pltpu.make_async_copy(ints.at[f], ints.at[f], in_sem.at[f]).wait()
        pltpu.make_async_copy(ints.at[f], int_out.at[f], out_sem.at[f]).start()
        total = jnp.zeros((rows, rows), F32)
        for r in range(0, dom * TB, rows):
            spot = pl.ds(r, rows)
            acc = lax.dot_general(ints[f, spot, :], amp[...], NT, preferred_element_type=F32)
            half[f, spot, :] = acc.astype(BF16)
            total = total + acc[:, r : r + rows]
            if not finish:
                pltpu.make_async_copy(
                    half.at[f, spot, :], out_ref.at[f, spot, :], out_sem.at[len(flips)]
                ).start()
        trace = jnp.sum(jnp.where(diagonal, total, 0.0))
        traces.append((which * CORES + flip, trace))
    load_inter.wait()
    inter = inter_ref[...]
    for place, trace in traces:
        inter = jnp.where(lane == place, trace, inter)
    inter_ref[...] = inter
    store_inter = pltpu.make_async_copy(inter_ref, inter_out, out_sem.at[len(flips) + 1])
    store_inter.start()
    if finish:
        for r in range(0, dom * TB, rows):
            spot = pl.ds(r, rows)
            acc = None
            for f in range(len(flips)):
                term = lax.dot_general(ints[f, spot, :], half[f], NT, preferred_element_type=F32)
                acc = term if acc is None else acc + term
            ladder[spot, :] = acc
            pltpu.make_async_copy(
                ladder.at[spot, :], out_ref.at[spot, :], out_sem.at[len(flips)]
            ).start()
    for f in range(len(flips)):
        pltpu.make_async_copy(ints.at[f], int_out.at[f], out_sem.at[f]).wait()
    pltpu.make_async_copy(ladder if finish else half, out_ref, out_sem.at[len(flips)]).wait()
    store_inter.wait()


def work(amp, before, parts, domain, here, which, flips, finish, quarter):
    length = amp.shape[0]
    count = len(flips)
    anywhere = pl.BlockSpec(memory_space=pl.ANY)
    squares = (count, length, length)
    return pl.pallas_call(
        functools.partial(work_kernel, quarter, domain.shape[1], which, flips, finish),
        out_shape=[
            jax.ShapeDtypeStruct(squares, BF16),
            jax.ShapeDtypeStruct((length, length), F32)
            if finish
            else jax.ShapeDtypeStruct(squares, BF16),
            jax.ShapeDtypeStruct(before.shape, F32),
        ],
        grid_spec=pltpu.PrefetchScalarGridSpec(
            num_scalar_prefetch=2,
            grid=(1,),
            in_specs=[anywhere] * (2 + len(parts)),
            out_specs=[anywhere] * 3,
            scratch_shapes=[
                pltpu.VMEM((length, length), BF16),
                pltpu.VMEM(squares, BF16),
                pltpu.VMEM(squares, BF16),
                pltpu.VMEM((length, length), F32),
                pltpu.VMEM(before.shape, F32),
                pltpu.SemaphoreType.DMA((count + 2,)),
                pltpu.SemaphoreType.DMA((count + 2,)),
            ],
        ),
        compiler_params=pltpu.CompilerParams(vmem_limit_bytes=VMEM_LIMIT),
        cost_estimate=pl.CostEstimate(
            flops=(4 if finish else 2) * count * length**3,
            bytes_accessed=10 * count * length**2,
            transcendentals=0,
        ),
        name="half_and_ladder" if finish else "half_ladder",
    )(domain, here, amp, before, *parts)


def ladder_kernel(int_ref, half_ref, before_ref, out_ref, ints, half, total, in_sem, out_sem):
    length = total.shape[0]
    rows = length // 3
    spots = [pl.ds(r, rows) for r in range(0, length, rows)]
    load_half = pltpu.make_async_copy(half_ref.at[0], half, in_sem.at[0])
    load_half.start()
    loads = []
    for n, spot in enumerate(spots):
        loads.append(
            [
                pltpu.make_async_copy(int_ref.at[0, spot, :], ints.at[spot, :], in_sem.at[2 * n + 1]),
                pltpu.make_async_copy(before_ref.at[spot, :], total.at[spot, :], in_sem.at[2 * n + 2]),
            ]
        )
        for load in loads[-1]:
            load.start()
    load_half.wait()
    for spot, pair_of_loads in zip(spots, loads):
        for load in pair_of_loads:
            load.wait()
        total[spot, :] += lax.dot_general(
            ints[spot, :], half[...], NT, preferred_element_type=F32
        )
        pltpu.make_async_copy(total.at[spot, :], out_ref.at[spot, :], out_sem.at[0]).start()
    pltpu.make_async_copy(total, out_ref, out_sem.at[0]).wait()


def ladder(ints, half, before):
    length = before.shape[0]
    anywhere = pl.BlockSpec(memory_space=pl.ANY)
    return pl.pallas_call(
        ladder_kernel,
        out_shape=jax.ShapeDtypeStruct((length, length), F32),
        in_specs=[anywhere] * 3,
        out_specs=anywhere,
        scratch_shapes=[
            pltpu.VMEM((length, length), BF16),
            pltpu.VMEM((length, length), BF16),
            pltpu.VMEM((length, length), F32),
            pltpu.SemaphoreType.DMA((7,)),
            pltpu.SemaphoreType.DMA((1,)),
        ],
        compiler_params=pltpu.CompilerParams(vmem_limit_bytes=VMEM_LIMIT),
        cost_estimate=pl.CostEstimate(
            flops=2 * length**3, bytes_accessed=12 * length**2, transcendentals=0
        ),
        name="ladder",
    )(ints, half, before)


def cycle_kernel(which, places, here_ref, coupling_ref, inter_ref, *rest):
    sources, rest = rest[: CORES + 1], rest[CORES + 1 :]
    count = (len(rest) - 4) // 2
    outs, kept, (ints, ladder, in_sem, out_sem) = rest[:count], rest[count : 2 * count], rest[2 * count :]
    y, x, core = here_ref[1], here_ref[2], here_ref[3]
    rows = outs[0].shape[1]
    ny, nx = (outs[0].shape[0], count) if which == 0 else (count, outs[0].shape[0])
    group = nx * rows
    loads = []
    for t in range(ny):
        spot = pl.ds(pl.multiple_of(lax.rem(y + t, ny) * group, group), group)
        loads.append(
            [
                pltpu.make_async_copy(
                    sources[f].at[places[f], spot, :], ints.at[f, t], in_sem.at[t * (CORES + 1) + f]
                )
                for f in range(CORES)
            ]
            + [
                pltpu.make_async_copy(
                    sources[CORES].at[spot, :], ladder.at[t], in_sem.at[t * (CORES + 1) + CORES]
                )
            ]
        )
        for load in loads[-1]:
            load.start()
    dressing = []
    for f in range(CORES):
        total = jnp.float32(0)
        for source in range(BLOCKS * CORES):
            flip = (source % CORES) ^ core ^ f
            for w in range(CORES):
                total = total + coupling_ref[core * CORES + which, source * CORES + w] * (
                    inter_ref[source, w * CORES + flip]
                )
        dressing.append(total)
    for t in range(ny):
        for load in loads[t]:
            load.wait()
        for k in range(nx):
            spot = pl.ds(pl.multiple_of(lax.rem(x + k, nx) * rows, rows), rows)
            total = ladder[t, spot, :]
            for f in range(CORES):
                total = total + dressing[f] * ints[f, t, spot, :].astype(F32)
            n, place = (k, t) if which == 0 else (t, k)
            kept[n][place] = total.astype(kept[n].dtype)
            if which == 0:
                pltpu.make_async_copy(kept[n].at[place], outs[n].at[place], out_sem.at[n]).start()
        if which == 1:
            pltpu.make_async_copy(kept[t], outs[t], out_sem.at[t]).start()
    for n in range(count):
        pltpu.make_async_copy(kept[n], outs[n], out_sem.at[n]).wait()


def add_cycle(ladder_sum, ints, inter, coupling, here, which, ny, nx):
    length = ladder_sum.shape[0]
    rows = length // (ny * nx)
    anywhere = pl.BlockSpec(memory_space=pl.ANY)
    count, shape = (nx, (ny, rows, length)) if which == 0 else (ny, (nx, rows, length))
    return pl.pallas_call(
        functools.partial(cycle_kernel, which, [place for _, place in ints]),
        out_shape=[jax.ShapeDtypeStruct(shape, BF16 if s else F32) for s in range(count)],
        grid_spec=pltpu.PrefetchScalarGridSpec(
            num_scalar_prefetch=3,
            grid=(1,),
            in_specs=[anywhere] * (CORES + 1),
            out_specs=[anywhere] * count,
            scratch_shapes=[pltpu.VMEM(shape, BF16 if s else F32) for s in range(count)]
            + [
                pltpu.VMEM((CORES, ny, nx * rows, length), BF16),
                pltpu.VMEM((ny, nx * rows, length), F32),
                pltpu.SemaphoreType.DMA((ny * (CORES + 1),)),
                pltpu.SemaphoreType.DMA((count,)),
            ],
        ),
        compiler_params=pltpu.CompilerParams(vmem_limit_bytes=VMEM_LIMIT),
        cost_estimate=pl.CostEstimate(
            flops=6 * length**2, bytes_accessed=12 * length**2, transcendentals=0
        ),
        name="add_cycle",
    )(here, coupling, inter, *(array for array, _ in ints), ladder_sum)


def sum_over(axis, size, parts):
    total = parts[0].astype(F32)
    for s in (1, 3, 2):
        perm = [(i, (i + s) % size) for i in range(size)]
        total = total + lax.ppermute(parts[s].astype(BF16), axis, perm).astype(F32)
    return total


def masked_amps(amps, pair_mask, first_row, dom):
    pairs, rows, length = amps.shape
    row_slot = (first_row + jnp.arange(rows, dtype=jnp.int32)) // TB
    slot_pick = row_slot[:, None] == jnp.arange(dom, dtype=jnp.int32)[None, :]
    row_tiles = jnp.sum(
        jnp.where(slot_pick[None, :, :, None], pair_mask[:, None, :, :], 0), axis=2
    ).astype(BF16)
    tiles = amps.reshape(pairs, rows, dom, TB) * row_tiles[:, :, :, None]
    return tiles.reshape(pairs, rows, length)


def by_core(core, mine, other, axis):
    return jnp.where(
        core == 0,
        jnp.concatenate([mine, other], axis=axis),
        jnp.concatenate([other, mine], axis=axis),
    )


def make_body(ny, nx):
    def gather(rows, chips):
        got = lax.all_to_all(
            jnp.broadcast_to(rows[None], (chips,) + rows.shape), ("y", "x"), 0, 0, tiled=True
        )
        return [got[:, i].reshape(chips * rows.shape[1], rows.shape[2]) for i in range(rows.shape[0])]

    def send(key, packed):
        return [
            part if (s, key[1]) == (0, 0) else hop(s, key[1])(part)
            for s, part in zip(SHIFTS, packed)
        ]

    def body(amps, domain, pair_mask, dfint, coupling):
        pairs, own, length = amps.shape
        dom = domain.shape[1]
        quarter = dfint.shape[1] // TB
        each = pairs // CORES
        chips = ny * nx
        z, y, x, c = (lax.axis_index(name).astype(jnp.int32) for name in ("z", "y", "x", "c"))
        here = jnp.stack([z, y, x, c])
        order = [(which, f) for which in range(each) for f in range(CORES)]
        packed = {order[0]: pack(dfint, domain, here, *order[0], quarter)}
        packed[order[0]], amps = lax.optimization_barrier((packed[order[0]], amps))
        for key in order[1:]:
            packed[key] = pack(dfint, domain, here, *key, quarter)
        masked = masked_amps(amps, pair_mask, ((y * nx + x) * CORES + c) * own, dom)
        mine = lax.dynamic_slice_in_dim(masked, c * each, each, axis=0)
        other = swap_cores(lax.dynamic_slice_in_dim(masked, (1 - c) * each, each, axis=0))
        both = by_core(c, mine, other, 1)
        parts = {}
        for key in order[:EARLY]:
            parts[key] = send(key, packed.pop(key))
        early = [parts[key][n] for key, n in FIRST]
        early, packed, both = lax.optimization_barrier((early, packed, both))
        for (key, n), part in zip(FIRST, early):
            parts[key][n] = part
        for key in order[EARLY:]:
            parts[key] = send(key, packed[key])
        amp = gather(both, chips)
        inter = jnp.zeros((BLOCKS * CORES, TB), F32)
        ints0, ladder0, inter = work(
            amp[0], inter, parts[0, 0] + parts[0, 1], domain, here, 0, (0, 1), True, quarter
        )
        ints1, ladder1, inter = work(
            amp[1], inter, parts[1, 0], domain, here, 1, (0,), True, quarter
        )
        ints2, half, inter = work(
            amp[1], inter, parts[1, 1], domain, here, 1, (1,), False, quarter
        )
        sums = [ladder0, ladder(ints2, half, ladder1)]
        blocks = [[(ints0, 0), (ints0, 1)], [(ints1, 0), (ints2, 0)]]
        every = lax.all_to_all(inter, ("z", "c"), 0, 0, tiled=True)
        ends = []
        for which in range(each):
            (first, n1), (second, n2) = (("x", nx), ("y", ny))[:: 1 if which == 0 else -1]
            parts_out = add_cycle(
                sums[which], blocks[which], every, coupling, here, which, ny, nx
            )
            stage = sum_over(first, n1, parts_out)
            ends.append(sum_over(second, n2, [stage[s] for s in range(n2)]))
        result = jnp.stack(ends).astype(BF16)
        mine = lax.dynamic_slice_in_dim(result, c * own, own, axis=1)
        other = swap_cores(lax.dynamic_slice_in_dim(result, (1 - c) * own, own, axis=1))
        return by_core(c, mine, other, 0)

    return body


def solution(mesh):
    ny = nx = 4
    grid = Mesh(mesh.devices.reshape(BLOCKS, ny, nx, CORES), ("z", "y", "x", "c"))
    virt = ("y", "x", "c")
    return jax.shard_map(
        make_body(ny, nx),
        mesh=grid,
        in_specs=(P("z", virt, None), P(), P("z", None, None), P(virt, "z", None), P("z", None)),
        out_specs=P("z", virt, None),
        check_vma=False,
    )
```

```python
import functools

import jax
import jax.numpy as jnp
from jax import lax
from jax.experimental import pallas as pl
from jax.experimental.pallas import tpu as pltpu
from jax.sharding import Mesh
from jax.sharding import PartitionSpec as P

TB = 128
BLOCKS = 4
CORES = 2
SLOTS = 2
VMEM_LIMIT = 56 * 2**20
BF16 = jnp.bfloat16
F32 = jnp.float32
NT = (((1,), (1,)), ((), ()))
SHIFTS = (1, 3, 2, 0)
EARLY = 1
FIRST = (((0, 0), 0), ((0, 0), 1), ((0, 0), 2))


def hop(shift, flip):
    perm = [
        (z * CORES + c, (z + shift) % BLOCKS * CORES + (c ^ flip))
        for z in range(BLOCKS)
        for c in range(CORES)
    ]
    return functools.partial(lax.ppermute, axis_name=("z", "c"), perm=perm)


def swap_cores(value):
    return lax.ppermute(value, "c", [(0, 1), (1, 0)])


def block_slots(domain_ref, pair, block, quarter, dom):
    found = jnp.int32(0)
    first = jnp.int32(0)
    second = jnp.int32(0)
    for s in range(dom):
        inside = domain_ref[pair, s] // quarter == block
        first = jnp.where(inside & (found == 0), s, first)
        second = jnp.where(inside & (found == 1), s, second)
        found = found + inside.astype(jnp.int32)
    return first, second


def pack_kernel(quarter, dom, which, flip, domain_ref, here_ref, dfint_ref, *rest):
    count = len(SHIFTS)
    outs, (buffer, in_sem, out_sem) = rest[:count], rest[count:]
    here, core = here_ref[0], here_ref[3]
    for n, shift in enumerate(SHIFTS):
        target = lax.rem(here + shift, BLOCKS)
        pair = (target * CORES + (core ^ flip)) * CORES + which
        for j, slot in enumerate(block_slots(domain_ref, pair, here, quarter, dom)):
            row = jnp.clip(domain_ref[pair, slot] - here * quarter, 0, quarter - 1)
            for t in range(dom):
                column = domain_ref[pair, t]
                pltpu.make_async_copy(
                    dfint_ref.at[
                        0,
                        pl.ds(pl.multiple_of(row * TB, TB), TB),
                        pl.ds(pl.multiple_of(column * TB, TB), TB),
                    ],
                    buffer.at[n, j, :, pl.ds(t * TB, TB)],
                    in_sem.at[n],
                ).start()
    for n in range(count):
        pltpu.make_async_copy(buffer.at[n], buffer.at[n], in_sem.at[n]).wait()
        pltpu.make_async_copy(buffer.at[n], outs[n], out_sem.at[n]).start()
    for n in range(count):
        pltpu.make_async_copy(buffer.at[n], outs[n], out_sem.at[n]).wait()


def pack(dfint, domain, here, which, flip, quarter):
    dom = domain.shape[1]
    count = len(SHIFTS)
    tile_rows = (SLOTS, TB, dom * TB)
    return pl.pallas_call(
        functools.partial(pack_kernel, quarter, dom, which, flip),
        out_shape=[jax.ShapeDtypeStruct(tile_rows, BF16)] * count,
        grid_spec=pltpu.PrefetchScalarGridSpec(
            num_scalar_prefetch=2,
            grid=(1,),
            in_specs=[pl.BlockSpec(memory_space=pl.ANY)],
            out_specs=[pl.BlockSpec(memory_space=pl.ANY)] * count,
            scratch_shapes=[
                pltpu.VMEM((count,) + tile_rows, BF16),
                pltpu.SemaphoreType.DMA((count,)),
                pltpu.SemaphoreType.DMA((count,)),
            ],
        ),
        compiler_params=pltpu.CompilerParams(vmem_limit_bytes=VMEM_LIMIT),
        cost_estimate=pl.CostEstimate(flops=12000000000, bytes_accessed=1, transcendentals=0),
        name="pack_tiles",
    )(domain, here, dfint)


def work_kernel(quarter, dom, which, flips, finish, domain_ref, here_ref, amp_ref, before_ref, *rest):
    count = len(SHIFTS)
    parts, rest = rest[: count * len(flips)], rest[count * len(flips) :]
    int_out, out_ref, inter_out, amp, ints, half, ladder, inter_ref, in_sem, out_sem = rest
    here, core = here_ref[0], here_ref[3]
    pair = (here * CORES + core) * CORES + which
    load_amp = pltpu.make_async_copy(amp_ref, amp, in_sem.at[len(flips)])
    load_amp.start()
    load_inter = pltpu.make_async_copy(before_ref, inter_ref, in_sem.at[len(flips) + 1])
    load_inter.start()
    for s in range(dom):
        owner = domain_ref[pair, s] // quarter
        rank = jnp.int32(0)
        for earlier in range(s):
            rank = rank + (domain_ref[pair, earlier] // quarter == owner).astype(jnp.int32)
        shift = lax.rem(here - owner + BLOCKS, BLOCKS)
        for n, flow_shift in enumerate(SHIFTS):

            @pl.when(shift == flow_shift)
            def _(n=n, rank=rank, s=s):
                for f in range(len(flips)):
                    pltpu.make_async_copy(
                        parts[f * count + n].at[rank],
                        ints.at[f, pl.ds(s * TB, TB), :],
                        in_sem.at[f],
                    ).start()

    load_amp.wait()
    rows = 2 * TB
    diagonal = lax.broadcasted_iota(jnp.int32, (rows, rows), 0) == lax.broadcasted_iota(
        jnp.int32, (rows, rows), 1
    )
    lane = lax.broadcasted_iota(jnp.int32, inter_ref.shape, 1)
    traces = []
    for f, flip in enumerate(flips):
        pltpu.make_async_copy(ints.at[f], ints.at[f], in_sem.at[f]).wait()
        pltpu.make_async_copy(ints.at[f], int_out.at[f], out_sem.at[f]).start()
        total = jnp.zeros((rows, rows), F32)
        for r in range(0, dom * TB, rows):
            spot = pl.ds(r, rows)
            acc = lax.dot_general(ints[f, spot, :], amp[...], NT, preferred_element_type=F32)
            half[f, spot, :] = acc.astype(BF16)
            total = total + acc[:, r : r + rows]
            if not finish:
                pltpu.make_async_copy(
                    half.at[f, spot, :], out_ref.at[f, spot, :], out_sem.at[len(flips)]
                ).start()
        trace = jnp.sum(jnp.where(diagonal, total, 0.0))
        traces.append((which * CORES + flip, trace))
    load_inter.wait()
    inter = inter_ref[...]
    for place, trace in traces:
        inter = jnp.where(lane == place, trace, inter)
    inter_ref[...] = inter
    store_inter = pltpu.make_async_copy(inter_ref, inter_out, out_sem.at[len(flips) + 1])
    store_inter.start()
    if finish:
        for r in range(0, dom * TB, rows):
            spot = pl.ds(r, rows)
            acc = None
            for f in range(len(flips)):
                term = lax.dot_general(ints[f, spot, :], half[f], NT, preferred_element_type=F32)
                acc = term if acc is None else acc + term
            ladder[spot, :] = acc
            pltpu.make_async_copy(
                ladder.at[spot, :], out_ref.at[spot, :], out_sem.at[len(flips)]
            ).start()
    for f in range(len(flips)):
        pltpu.make_async_copy(ints.at[f], int_out.at[f], out_sem.at[f]).wait()
    pltpu.make_async_copy(ladder if finish else half, out_ref, out_sem.at[len(flips)]).wait()
    store_inter.wait()


def work(amp, before, parts, domain, here, which, flips, finish, quarter):
    length = amp.shape[0]
    count = len(flips)
    anywhere = pl.BlockSpec(memory_space=pl.ANY)
    squares = (count, length, length)
    return pl.pallas_call(
        functools.partial(work_kernel, quarter, domain.shape[1], which, flips, finish),
        out_shape=[
            jax.ShapeDtypeStruct(squares, BF16),
            jax.ShapeDtypeStruct((length, length), F32)
            if finish
            else jax.ShapeDtypeStruct(squares, BF16),
            jax.ShapeDtypeStruct(before.shape, F32),
        ],
        grid_spec=pltpu.PrefetchScalarGridSpec(
            num_scalar_prefetch=2,
            grid=(1,),
            in_specs=[anywhere] * (2 + len(parts)),
            out_specs=[anywhere] * 3,
            scratch_shapes=[
                pltpu.VMEM((length, length), BF16),
                pltpu.VMEM(squares, BF16),
                pltpu.VMEM(squares, BF16),
                pltpu.VMEM((length, length), F32),
                pltpu.VMEM(before.shape, F32),
                pltpu.SemaphoreType.DMA((count + 2,)),
                pltpu.SemaphoreType.DMA((count + 2,)),
            ],
        ),
        compiler_params=pltpu.CompilerParams(vmem_limit_bytes=VMEM_LIMIT),
        cost_estimate=pl.CostEstimate(flops=1, bytes_accessed=1, transcendentals=0),
        name="half_and_ladder" if finish else "half_ladder",
    )(domain, here, amp, before, *parts)


def ladder_kernel(int_ref, half_ref, before_ref, out_ref, ints, half, total, in_sem, out_sem):
    length = total.shape[0]
    rows = length // 3
    spots = [pl.ds(r, rows) for r in range(0, length, rows)]
    load_half = pltpu.make_async_copy(half_ref.at[0], half, in_sem.at[0])
    load_half.start()
    loads = []
    for n, spot in enumerate(spots):
        loads.append(
            [
                pltpu.make_async_copy(int_ref.at[0, spot, :], ints.at[spot, :], in_sem.at[2 * n + 1]),
                pltpu.make_async_copy(before_ref.at[spot, :], total.at[spot, :], in_sem.at[2 * n + 2]),
            ]
        )
        for load in loads[-1]:
            load.start()
    load_half.wait()
    for spot, pair_of_loads in zip(spots, loads):
        for load in pair_of_loads:
            load.wait()
        total[spot, :] += lax.dot_general(
            ints[spot, :], half[...], NT, preferred_element_type=F32
        )
        pltpu.make_async_copy(total.at[spot, :], out_ref.at[spot, :], out_sem.at[0]).start()
    pltpu.make_async_copy(total, out_ref, out_sem.at[0]).wait()


def ladder(ints, half, before):
    length = before.shape[0]
    anywhere = pl.BlockSpec(memory_space=pl.ANY)
    return pl.pallas_call(
        ladder_kernel,
        out_shape=jax.ShapeDtypeStruct((length, length), F32),
        in_specs=[anywhere] * 3,
        out_specs=anywhere,
        scratch_shapes=[
            pltpu.VMEM((length, length), BF16),
            pltpu.VMEM((length, length), BF16),
            pltpu.VMEM((length, length), F32),
            pltpu.SemaphoreType.DMA((7,)),
            pltpu.SemaphoreType.DMA((1,)),
        ],
        compiler_params=pltpu.CompilerParams(vmem_limit_bytes=VMEM_LIMIT),
        cost_estimate=pl.CostEstimate(flops=1, bytes_accessed=1, transcendentals=0),
        name="ladder",
    )(ints, half, before)


def cycle_kernel(which, places, here_ref, coupling_ref, inter_ref, *rest):
    sources, rest = rest[: CORES + 1], rest[CORES + 1 :]
    count = (len(rest) - 4) // 2
    outs, kept, (ints, ladder, in_sem, out_sem) = rest[:count], rest[count : 2 * count], rest[2 * count :]
    y, x, core = here_ref[1], here_ref[2], here_ref[3]
    rows = outs[0].shape[1]
    ny, nx = (outs[0].shape[0], count) if which == 0 else (count, outs[0].shape[0])
    group = nx * rows
    loads = []
    for t in range(ny):
        spot = pl.ds(pl.multiple_of(lax.rem(y + t, ny) * group, group), group)
        loads.append(
            [
                pltpu.make_async_copy(
                    sources[f].at[places[f], spot, :], ints.at[f, t], in_sem.at[t * (CORES + 1) + f]
                )
                for f in range(CORES)
            ]
            + [
                pltpu.make_async_copy(
                    sources[CORES].at[spot, :], ladder.at[t], in_sem.at[t * (CORES + 1) + CORES]
                )
            ]
        )
        for load in loads[-1]:
            load.start()
    dressing = []
    for f in range(CORES):
        total = jnp.float32(0)
        for source in range(BLOCKS * CORES):
            flip = (source % CORES) ^ core ^ f
            for w in range(CORES):
                total = total + coupling_ref[core * CORES + which, source * CORES + w] * (
                    inter_ref[source, w * CORES + flip]
                )
        dressing.append(total)
    for t in range(ny):
        for load in loads[t]:
            load.wait()
        for k in range(nx):
            spot = pl.ds(pl.multiple_of(lax.rem(x + k, nx) * rows, rows), rows)
            total = ladder[t, spot, :]
            for f in range(CORES):
                total = total + dressing[f] * ints[f, t, spot, :].astype(F32)
            n, place = (k, t) if which == 0 else (t, k)
            kept[n][place] = total.astype(kept[n].dtype)
            if which == 0:
                pltpu.make_async_copy(kept[n].at[place], outs[n].at[place], out_sem.at[n]).start()
        if which == 1:
            pltpu.make_async_copy(kept[t], outs[t], out_sem.at[t]).start()
    for n in range(count):
        pltpu.make_async_copy(kept[n], outs[n], out_sem.at[n]).wait()


def add_cycle(ladder_sum, ints, inter, coupling, here, which, ny, nx):
    length = ladder_sum.shape[0]
    rows = length // (ny * nx)
    anywhere = pl.BlockSpec(memory_space=pl.ANY)
    count, shape = (nx, (ny, rows, length)) if which == 0 else (ny, (nx, rows, length))
    return pl.pallas_call(
        functools.partial(cycle_kernel, which, [place for _, place in ints]),
        out_shape=[jax.ShapeDtypeStruct(shape, BF16 if s else F32) for s in range(count)],
        grid_spec=pltpu.PrefetchScalarGridSpec(
            num_scalar_prefetch=3,
            grid=(1,),
            in_specs=[anywhere] * (CORES + 1),
            out_specs=[anywhere] * count,
            scratch_shapes=[pltpu.VMEM(shape, BF16 if s else F32) for s in range(count)]
            + [
                pltpu.VMEM((CORES, ny, nx * rows, length), BF16),
                pltpu.VMEM((ny, nx * rows, length), F32),
                pltpu.SemaphoreType.DMA((ny * (CORES + 1),)),
                pltpu.SemaphoreType.DMA((count,)),
            ],
        ),
        compiler_params=pltpu.CompilerParams(vmem_limit_bytes=VMEM_LIMIT),
        cost_estimate=pl.CostEstimate(flops=1, bytes_accessed=1, transcendentals=0),
        name="add_cycle",
    )(here, coupling, inter, *(array for array, _ in ints), ladder_sum)


def sum_over(axis, size, parts):
    total = parts[0].astype(F32)
    for s in (1, 3, 2):
        perm = [(i, (i + s) % size) for i in range(size)]
        total = total + lax.ppermute(parts[s].astype(BF16), axis, perm).astype(F32)
    return total


def masked_amps(amps, pair_mask, first_row, dom):
    pairs, rows, length = amps.shape
    row_slot = (first_row + jnp.arange(rows, dtype=jnp.int32)) // TB
    slot_pick = row_slot[:, None] == jnp.arange(dom, dtype=jnp.int32)[None, :]
    row_tiles = jnp.sum(
        jnp.where(slot_pick[None, :, :, None], pair_mask[:, None, :, :], 0), axis=2
    ).astype(BF16)
    tiles = amps.reshape(pairs, rows, dom, TB) * row_tiles[:, :, :, None]
    return tiles.reshape(pairs, rows, length)


def by_core(core, mine, other, axis):
    return jnp.where(
        core == 0,
        jnp.concatenate([mine, other], axis=axis),
        jnp.concatenate([other, mine], axis=axis),
    )


def make_body(ny, nx):
    def gather(rows, chips):
        got = lax.all_to_all(
            jnp.broadcast_to(rows[None], (chips,) + rows.shape), ("y", "x"), 0, 0, tiled=True
        )
        return [got[:, i].reshape(chips * rows.shape[1], rows.shape[2]) for i in range(rows.shape[0])]

    def send(key, packed):
        return [
            part if (s, key[1]) == (0, 0) else hop(s, key[1])(part)
            for s, part in zip(SHIFTS, packed)
        ]

    def body(amps, domain, pair_mask, dfint, coupling):
        pairs, own, length = amps.shape
        dom = domain.shape[1]
        quarter = dfint.shape[1] // TB
        each = pairs // CORES
        chips = ny * nx
        z, y, x, c = (lax.axis_index(name).astype(jnp.int32) for name in ("z", "y", "x", "c"))
        here = jnp.stack([z, y, x, c])
        order = [(which, f) for which in range(each) for f in range(CORES)]
        packed = {order[0]: pack(dfint, domain, here, *order[0], quarter)}
        for key in order[1:]:
            packed[key] = pack(dfint, domain, here, *key, quarter)
        masked = masked_amps(amps, pair_mask, ((y * nx + x) * CORES + c) * own, dom)
        mine = lax.dynamic_slice_in_dim(masked, c * each, each, axis=0)
        other = swap_cores(lax.dynamic_slice_in_dim(masked, (1 - c) * each, each, axis=0))
        both = by_core(c, mine, other, 1)
        parts = {}
        for key in order[:EARLY]:
            parts[key] = send(key, packed.pop(key))
        early = [parts[key][n] for key, n in FIRST]
        early = early
        for (key, n), part in zip(FIRST, early):
            parts[key][n] = part
        for key in order[EARLY:]:
            parts[key] = send(key, packed[key])
        amp = gather(both, chips)
        inter = jnp.zeros((BLOCKS * CORES, TB), F32)
        ints0, ladder0, inter = work(
            amp[0], inter, parts[0, 0] + parts[0, 1], domain, here, 0, (0, 1), True, quarter
        )
        ints1, ladder1, inter = work(
            amp[1], inter, parts[1, 0], domain, here, 1, (0,), True, quarter
        )
        ints2, half, inter = work(
            amp[1], inter, parts[1, 1], domain, here, 1, (1,), False, quarter
        )
        sums = [ladder0, ladder(ints2, half, ladder1)]
        blocks = [[(ints0, 0), (ints0, 1)], [(ints1, 0), (ints2, 0)]]
        every = lax.all_to_all(inter, ("z", "c"), 0, 0, tiled=True)
        ends = []
        for which in range(each):
            (first, n1), (second, n2) = (("x", nx), ("y", ny))[:: 1 if which == 0 else -1]
            parts_out = add_cycle(
                sums[which], blocks[which], every, coupling, here, which, ny, nx
            )
            stage = sum_over(first, n1, parts_out)
            ends.append(sum_over(second, n2, [stage[s] for s in range(n2)]))
        result = jnp.stack(ends).astype(BF16)
        mine = lax.dynamic_slice_in_dim(result, c * own, own, axis=1)
        other = swap_cores(lax.dynamic_slice_in_dim(result, (1 - c) * own, own, axis=1))
        return by_core(c, mine, other, 0)

    return body


def solution(mesh):
    ny = nx = 4
    grid = Mesh(mesh.devices.reshape(BLOCKS, ny, nx, CORES), ("z", "y", "x", "c"))
    virt = ("y", "x", "c")
    return jax.shard_map(
        make_body(ny, nx),
        mesh=grid,
        in_specs=(P("z", virt, None), P(), P("z", None, None), P(virt, "z", None), P("z", None)),
        out_specs=P("z", virt, None),
        check_vma=False,
    )
```

```python
import functools

import jax
import jax.numpy as jnp
from jax import lax
from jax.experimental import pallas as pl
from jax.experimental.pallas import tpu as pltpu
from jax.sharding import Mesh
from jax.sharding import PartitionSpec as P

TB = 128
BLOCKS = 4
RING = 4
CORES = 2
SLOTS = 2
VMEM_LIMIT = 56 * 2**20
BF16 = jnp.bfloat16
F32 = jnp.float32
NT = (((1,), (1,)), ((), ()))
SHIFTS = (1, 3, 2, 0)


def hop(shift, flip):
    perm = [
        (z * CORES + c, (z + shift) % BLOCKS * CORES + (c ^ flip))
        for z in range(BLOCKS)
        for c in range(CORES)
    ]
    return functools.partial(lax.ppermute, axis_name=("z", "c"), perm=perm)


def swap_cores(value):
    return lax.ppermute(value, "c", [(0, 1), (1, 0)])


def block_slots(scalars_ref, pair, block, quarter, dom):
    found = jnp.int32(0)
    first = jnp.int32(0)
    second = jnp.int32(0)
    for s in range(dom):
        inside = scalars_ref[pair * dom + s] // quarter == block
        first = jnp.where(inside & (found == 0), s, first)
        second = jnp.where(inside & (found == 1), s, second)
        found = found + inside.astype(jnp.int32)
    return first, second


def pack_kernel(quarter, dom, which, flip, scalars_ref, dfint_ref, *rest):
    count = len(SHIFTS)
    outs, (buffer, in_sem, out_sem) = rest[:count], rest[count:]
    here, core = (scalars_ref[scalars_ref.shape[0] - n] for n in (4, 1))
    for n, shift in enumerate(SHIFTS):
        target = lax.rem(here + shift, BLOCKS)
        pair = (target * CORES + (core ^ flip)) * CORES + which
        for j, slot in enumerate(block_slots(scalars_ref, pair, here, quarter, dom)):
            row = jnp.clip(scalars_ref[pair * dom + slot] - here * quarter, 0, quarter - 1)
            for t in range(dom):
                column = scalars_ref[pair * dom + t]
                pltpu.make_async_copy(
                    dfint_ref.at[
                        0,
                        pl.ds(pl.multiple_of(row * TB, TB), TB),
                        pl.ds(pl.multiple_of(column * TB, TB), TB),
                    ],
                    buffer.at[n, j, :, pl.ds(t * TB, TB)],
                    in_sem.at[n],
                ).start()
    for n in range(count):
        pltpu.make_async_copy(buffer.at[n], buffer.at[n], in_sem.at[n]).wait()
        pltpu.make_async_copy(buffer.at[n], outs[n], out_sem.at[n]).start()
    for n in range(count):
        pltpu.make_async_copy(buffer.at[n], outs[n], out_sem.at[n]).wait()


def pack(dfint, scalars, which, flip, quarter, dom):
    count = len(SHIFTS)
    tile_rows = (SLOTS, TB, dom * TB)
    return pl.pallas_call(
        functools.partial(pack_kernel, quarter, dom, which, flip),
        out_shape=[jax.ShapeDtypeStruct(tile_rows, BF16)] * count,
        grid_spec=pltpu.PrefetchScalarGridSpec(
            num_scalar_prefetch=1,
            grid=(1,),
            in_specs=[pl.BlockSpec(memory_space=pl.ANY)],
            out_specs=[pl.BlockSpec(memory_space=pl.ANY)] * count,
            scratch_shapes=[
                pltpu.VMEM((count,) + tile_rows, BF16),
                pltpu.SemaphoreType.DMA((count,)),
                pltpu.SemaphoreType.DMA((count,)),
            ],
        ),
        compiler_params=pltpu.CompilerParams(vmem_limit_bytes=VMEM_LIMIT),
        cost_estimate=pl.CostEstimate(flops=12000000000, bytes_accessed=1, transcendentals=0),
        name="pack_tiles",
    )(scalars, dfint)


def work_kernel(quarter, dom, jobs, finish, first, scalars_ref, amp_ref, *rest):
    count = len(SHIFTS)
    slots = [(which, flip) for which, flips in jobs for flip in flips]
    before_ref, rest = (None, rest) if first else (rest[0], rest[1:])
    parts, rest = rest[: count * len(slots)], rest[count * len(slots) :]
    int_out, results, inter_out = rest[0], rest[1 : 1 + len(jobs)], rest[1 + len(jobs)]
    amp, ints, half, ladder, inter_ref, amp_sem, in_sem, out_sem, small_sem = rest[2 + len(jobs) :]
    here, core = (scalars_ref[scalars_ref.shape[0] - n] for n in (4, 1))
    chip_rows = amp_ref.shape[2]
    if not first:
        load_inter = pltpu.make_async_copy(before_ref, inter_ref, small_sem.at[0])
        load_inter.start()
    slot = 0
    for job, (which, flips) in enumerate(jobs):
        for chip in range(amp_ref.shape[0]):
            pltpu.make_async_copy(
                amp_ref.at[chip, which],
                amp.at[job, pl.ds(chip * chip_rows, chip_rows), :],
                amp_sem.at[job],
            ).start()
        pair = (here * CORES + core) * CORES + which
        for s in range(dom):
            owner = scalars_ref[pair * dom + s] // quarter
            rank = jnp.int32(0)
            for earlier in range(s):
                rank = rank + (scalars_ref[pair * dom + earlier] // quarter == owner).astype(jnp.int32)
            shift = lax.rem(here - owner + BLOCKS, BLOCKS)
            for n, flow_shift in enumerate(SHIFTS):

                @pl.when(shift == flow_shift)
                def _(n=n, rank=rank, s=s, slot=slot, flips=flips):
                    for f in range(len(flips)):
                        pltpu.make_async_copy(
                            parts[(slot + f) * count + n].at[rank],
                            ints.at[slot + f, pl.ds(s * TB, TB), :],
                            in_sem.at[slot + f],
                        ).start()

        slot += len(flips)
    rows = 2 * TB
    diagonal = lax.broadcasted_iota(jnp.int32, (rows, rows), 0) == lax.broadcasted_iota(
        jnp.int32, (rows, rows), 1
    )
    traces = []
    slot = 0
    for job, (which, flips) in enumerate(jobs):
        pltpu.make_async_copy(amp.at[job], amp.at[job], amp_sem.at[job]).wait()
        for f, flip in enumerate(flips):
            place = slot + f
            pltpu.make_async_copy(ints.at[place], ints.at[place], in_sem.at[place]).wait()
            pltpu.make_async_copy(ints.at[place], int_out.at[place], out_sem.at[place]).start()
            total = jnp.zeros((rows, rows), F32)
            for r in range(0, dom * TB, rows):
                spot = pl.ds(r, rows)
                acc = lax.dot_general(ints[place, spot, :], amp[job], NT, preferred_element_type=F32)
                half[place, spot, :] = acc.astype(BF16)
                total = total + acc[:, r : r + rows]
                if not finish:
                    pltpu.make_async_copy(
                        half.at[place, spot, :], results[job].at[f, spot, :], out_sem.at[len(slots) + job]
                    ).start()
            traces.append((which * CORES + flip, jnp.sum(jnp.where(diagonal, total, 0.0))))
        if finish:
            for r in range(0, dom * TB, rows):
                spot = pl.ds(r, rows)
                acc = None
                for place in range(slot, slot + len(flips)):
                    term = lax.dot_general(
                        ints[place, spot, :], half[place], NT, preferred_element_type=F32
                    )
                    acc = term if acc is None else acc + term
                ladder[job, spot, :] = acc
                pltpu.make_async_copy(
                    ladder.at[job, spot, :], results[job].at[spot, :], out_sem.at[len(slots) + job]
                ).start()
        slot += len(flips)
    if first:
        inter = jnp.zeros(inter_ref.shape, F32)
    else:
        load_inter.wait()
        inter = inter_ref[...]
    lane = lax.broadcasted_iota(jnp.int32, inter_ref.shape, 1)
    for place, trace in traces:
        inter = jnp.where(lane == place, trace, inter)
    inter_ref[...] = inter
    store_inter = pltpu.make_async_copy(inter_ref, inter_out, small_sem.at[1])
    store_inter.start()
    for place in range(len(slots)):
        pltpu.make_async_copy(ints.at[place], int_out.at[place], out_sem.at[place]).wait()
    for job in range(len(jobs)):
        done = ladder.at[job] if finish else half
        pltpu.make_async_copy(done, results[job], out_sem.at[len(slots) + job]).wait()
    store_inter.wait()


def work(amp, before, parts, scalars, jobs, finish, quarter, dom):
    length = amp.shape[-1]
    count = sum(len(flips) for _, flips in jobs)
    anywhere = pl.BlockSpec(memory_space=pl.ANY)
    squares = (count, length, length)
    inter_shape = (BLOCKS * CORES, TB)
    result = jax.ShapeDtypeStruct((length, length), F32) if finish else jax.ShapeDtypeStruct(squares, BF16)
    first = before is None
    operands = [amp] + ([] if first else [before]) + list(parts)
    return pl.pallas_call(
        functools.partial(work_kernel, quarter, dom, jobs, finish, first),
        out_shape=[jax.ShapeDtypeStruct(squares, BF16)]
        + [result] * len(jobs)
        + [jax.ShapeDtypeStruct(inter_shape, F32)],
        grid_spec=pltpu.PrefetchScalarGridSpec(
            num_scalar_prefetch=1,
            grid=(1,),
            in_specs=[anywhere] * len(operands),
            out_specs=[anywhere] * (2 + len(jobs)),
            scratch_shapes=[
                pltpu.VMEM((len(jobs), length, length), BF16),
                pltpu.VMEM(squares, BF16),
                pltpu.VMEM(squares, BF16),
                pltpu.VMEM((len(jobs), length, length) if finish else (1, 8, TB), F32),
                pltpu.VMEM(inter_shape, F32),
                pltpu.SemaphoreType.DMA((len(jobs),)),
                pltpu.SemaphoreType.DMA((count,)),
                pltpu.SemaphoreType.DMA((count + len(jobs),)),
                pltpu.SemaphoreType.DMA((2,)),
            ],
        ),
        compiler_params=pltpu.CompilerParams(vmem_limit_bytes=VMEM_LIMIT),
        cost_estimate=pl.CostEstimate(flops=1, bytes_accessed=1, transcendentals=0),
        name="half_and_ladder" if finish else "half_ladder",
    )(scalars, *operands)


def ladder_kernel(int_ref, half_ref, before_ref, out_ref, ints, half, total, in_sem, out_sem):
    length = total.shape[0]
    rows = length // 3
    spots = [pl.ds(r, rows) for r in range(0, length, rows)]
    load_half = pltpu.make_async_copy(half_ref.at[0], half, in_sem.at[0])
    load_half.start()
    loads = []
    for n, spot in enumerate(spots):
        loads.append(
            [
                pltpu.make_async_copy(int_ref.at[0, spot, :], ints.at[spot, :], in_sem.at[2 * n + 1]),
                pltpu.make_async_copy(before_ref.at[spot, :], total.at[spot, :], in_sem.at[2 * n + 2]),
            ]
        )
        for load in loads[-1]:
            load.start()
    load_half.wait()
    for spot, pair_of_loads in zip(spots, loads):
        for load in pair_of_loads:
            load.wait()
        total[spot, :] += lax.dot_general(
            ints[spot, :], half[...], NT, preferred_element_type=F32
        )
        pltpu.make_async_copy(total.at[spot, :], out_ref.at[spot, :], out_sem.at[0]).start()
    pltpu.make_async_copy(total, out_ref, out_sem.at[0]).wait()


def ladder(ints, half, before):
    length = before.shape[0]
    anywhere = pl.BlockSpec(memory_space=pl.ANY)
    return pl.pallas_call(
        ladder_kernel,
        out_shape=jax.ShapeDtypeStruct((length, length), F32),
        in_specs=[anywhere] * 3,
        out_specs=anywhere,
        scratch_shapes=[
            pltpu.VMEM((length, length), BF16),
            pltpu.VMEM((length, length), BF16),
            pltpu.VMEM((length, length), F32),
            pltpu.SemaphoreType.DMA((7,)),
            pltpu.SemaphoreType.DMA((1,)),
        ],
        compiler_params=pltpu.CompilerParams(vmem_limit_bytes=VMEM_LIMIT),
        cost_estimate=pl.CostEstimate(flops=1, bytes_accessed=1, transcendentals=0),
        name="ladder",
    )(ints, half, before)


def cycle_kernel(places, scalars_ref, coupling_ref, inter_ref, *rest):
    each = len(places)
    width = CORES + 1
    sources, rest = rest[: each * width], rest[each * width :]
    count = (len(rest) - 4) // 2
    outs, kept, (ints, ladder, in_sem, out_sem) = rest[:count], rest[count : 2 * count], rest[2 * count :]
    y, x, core = (scalars_ref[scalars_ref.shape[0] - n] for n in (3, 2, 1))
    rows = outs[0].shape[1]
    group = RING * rows
    loads = {}
    for which in range(each):
        for t in range(RING):
            spot = pl.ds(pl.multiple_of(lax.rem(y + t, RING) * group, group), group)
            sem = (which * RING + t) * width
            loads[which, t] = [
                pltpu.make_async_copy(
                    sources[which * width + f].at[places[which][f], spot, :],
                    ints.at[which, f, t],
                    in_sem.at[sem + f],
                )
                for f in range(CORES)
            ]
            loads[which, t].append(
                pltpu.make_async_copy(
                    sources[which * width + CORES].at[spot, :],
                    ladder.at[which, t],
                    in_sem.at[sem + CORES],
                )
            )
            for load in loads[which, t]:
                load.start()
    dressing = {}
    for which in range(each):
        for f in range(CORES):
            total = jnp.float32(0)
            for source in range(BLOCKS * CORES):
                flip = (source % CORES) ^ core ^ f
                for w in range(CORES):
                    total = total + coupling_ref[core * CORES + which, source * CORES + w] * (
                        inter_ref[source, w * CORES + flip]
                    )
            dressing[which, f] = total
    for which in range(each):
        for t in range(RING):
            for load in loads[which, t]:
                load.wait()
            for k in range(RING):
                spot = pl.ds(pl.multiple_of(lax.rem(x + k, RING) * rows, rows), rows)
                total = ladder[which, t, spot, :]
                for f in range(CORES):
                    total = total + dressing[which, f] * ints[which, f, t, spot, :].astype(F32)
                n, place = (k, t) if which == 0 else (RING + t, k)
                kept[n][place] = total.astype(kept[n].dtype)
                pltpu.make_async_copy(kept[n].at[place], outs[n].at[place], out_sem.at[n]).start()
    for n in range(count):
        pltpu.make_async_copy(kept[n], outs[n], out_sem.at[n]).wait()


def add_cycle(sums, blocks, inter, coupling, scalars):
    each = len(sums)
    length = sums[0].shape[0]
    rows = length // RING**2
    anywhere = pl.BlockSpec(memory_space=pl.ANY)
    shape = (RING, rows, length)
    dtypes = [BF16 if s else F32 for s in range(RING)] * each
    sources = []
    for ints, ladder_sum in zip(blocks, sums):
        sources += [array for array, _ in ints] + [ladder_sum]
    outs = pl.pallas_call(
        functools.partial(cycle_kernel, [[place for _, place in ints] for ints in blocks]),
        out_shape=[jax.ShapeDtypeStruct(shape, dtype) for dtype in dtypes],
        grid_spec=pltpu.PrefetchScalarGridSpec(
            num_scalar_prefetch=3,
            grid=(1,),
            in_specs=[anywhere] * len(sources),
            out_specs=[anywhere] * len(dtypes),
            scratch_shapes=[pltpu.VMEM(shape, dtype) for dtype in dtypes]
            + [
                pltpu.VMEM((each, CORES, RING, RING * rows, length), BF16),
                pltpu.VMEM((each, RING, RING * rows, length), F32),
                pltpu.SemaphoreType.DMA((each * RING * (CORES + 1),)),
                pltpu.SemaphoreType.DMA((len(dtypes),)),
            ],
        ),
        compiler_params=pltpu.CompilerParams(vmem_limit_bytes=VMEM_LIMIT),
        cost_estimate=pl.CostEstimate(flops=1, bytes_accessed=1, transcendentals=0),
        name="add_cycle",
    )(scalars, coupling, inter, *sources)
    return [outs[which * RING : (which + 1) * RING] for which in range(each)]


def sum_over(axis, parts):
    total = parts[0].astype(F32)
    for s in (1, 3, 2):
        perm = [(i, (i + s) % RING) for i in range(RING)]
        total = total + lax.ppermute(parts[s].astype(BF16), axis, perm).astype(F32)
    return total


def masked_amps(amps, pair_mask, first_row, dom):
    pairs, rows, length = amps.shape
    row_slot = (first_row + jnp.arange(rows, dtype=jnp.int32)) // TB
    slot_pick = row_slot[:, None] == jnp.arange(dom, dtype=jnp.int32)[None, :]
    row_tiles = jnp.sum(
        jnp.where(slot_pick[None, :, :, None], pair_mask[:, None, :, :], 0), axis=2
    ).astype(BF16)
    tiles = amps.reshape(pairs, rows, dom, TB) * row_tiles[:, :, :, None]
    return tiles.reshape(pairs, rows, length)


def by_core(core, mine, other, axis):
    return jnp.where(
        core == 0,
        jnp.concatenate([mine, other], axis=axis),
        jnp.concatenate([other, mine], axis=axis),
    )


def make_body(ny, nx):
    def send(key, packed):
        return [
            part if (s, key[1]) == (0, 0) else hop(s, key[1])(part)
            for s, part in zip(SHIFTS, packed)
        ]

    def body(amps, domain, pair_mask, dfint, coupling):
        pairs, own, length = amps.shape
        dom = domain.shape[1]
        quarter = dfint.shape[1] // TB
        each = pairs // CORES
        chips = ny * nx
        z, y, x, c = (lax.axis_index(name).astype(jnp.int32) for name in ("z", "y", "x", "c"))
        scalars = jnp.concatenate([domain.reshape(-1), jnp.stack([z, y, x, c])])
        order = [(which, f) for which in range(each) for f in range(CORES)]
        packed = {order[0]: pack(dfint, scalars, *order[0], quarter, dom)}
        for key in order[1:]:
            packed[key] = pack(dfint, scalars, *key, quarter, dom)
        (packed[1, 0], amps, pair_mask) = lax.optimization_barrier((packed[1, 0], amps, pair_mask))
        masked = masked_amps(amps, pair_mask, ((y * nx + x) * CORES + c) * own, dom)
        mine = lax.dynamic_slice_in_dim(masked, c * each, each, axis=0)
        other = swap_cores(lax.dynamic_slice_in_dim(masked, (1 - c) * each, each, axis=0))
        both = by_core(c, mine, other, 1)
        amp = lax.all_to_all(
            jnp.broadcast_to(both[None], (chips,) + both.shape), ("y", "x"), 0, 0, tiled=True
        )
        parts = {key: send(key, packed[key]) for key in order[:-1]}
        parts[order[-1]] = send(order[-1], packed[order[-1]])
        ints, ladder0, ladder1, inter = work(
            amp,
            None,
            parts[0, 0] + parts[0, 1] + parts[1, 0],
            scalars,
            ((0, (0, 1)), (1, (0,))),
            True,
            quarter,
            dom,
        )
        late, half, inter = work(
            amp, inter, parts[1, 1], scalars, ((1, (1,)),), False, quarter, dom
        )
        sums = [ladder0, ladder(late, half, ladder1)]
        blocks = [[(ints, 0), (ints, 1)], [(ints, 2), (late, 0)]]
        every = lax.all_to_all(inter, ("z", "c"), 0, 0, tiled=True)
        ends = []
        for ordered, (first, second) in zip(
            add_cycle(sums, blocks, every, coupling, scalars), (("x", "y"), ("y", "x"))
        ):
            stage = sum_over(first, ordered)
            ends.append(sum_over(second, [stage[s] for s in range(RING)]))
        result = jnp.stack(ends).astype(BF16)
        mine = lax.dynamic_slice_in_dim(result, c * own, own, axis=1)
        other = swap_cores(lax.dynamic_slice_in_dim(result, (1 - c) * own, own, axis=1))
        return by_core(c, mine, other, 0)

    return body


def solution(mesh):
    ny = nx = 4
    grid = Mesh(mesh.devices.reshape(BLOCKS, ny, nx, CORES), ("z", "y", "x", "c"))
    virt = ("y", "x", "c")
    return jax.shard_map(
        make_body(ny, nx),
        mesh=grid,
        in_specs=(P("z", virt, None), P(), P("z", None, None), P(virt, "z", None), P("z", None)),
        out_specs=P("z", virt, None),
        check_vma=False,
    )
```

```python
import functools

import jax
import jax.numpy as jnp
from jax import lax
from jax.experimental import pallas as pl
from jax.experimental.pallas import tpu as pltpu
from jax.sharding import Mesh
from jax.sharding import PartitionSpec as P

TB = 128
BLOCKS = 4
RING = 4
CORES = 2
SLOTS = 2
VMEM_LIMIT = 56 * 2**20
BF16 = jnp.bfloat16
F32 = jnp.float32
NT = (((1,), (1,)), ((), ()))
SHIFTS = (1, 3, 2, 0)


def hop(shift, flip):
    perm = [
        (z * CORES + c, (z + shift) % BLOCKS * CORES + (c ^ flip))
        for z in range(BLOCKS)
        for c in range(CORES)
    ]
    return functools.partial(lax.ppermute, axis_name=("z", "c"), perm=perm)


def swap_cores(value):
    return lax.ppermute(value, "c", [(0, 1), (1, 0)])


def block_slots(scalars_ref, pair, block, quarter, dom):
    found = jnp.int32(0)
    first = jnp.int32(0)
    second = jnp.int32(0)
    for s in range(dom):
        inside = scalars_ref[pair * dom + s] // quarter == block
        first = jnp.where(inside & (found == 0), s, first)
        second = jnp.where(inside & (found == 1), s, second)
        found = found + inside.astype(jnp.int32)
    return first, second


def pack_kernel(quarter, dom, which, flip, scalars_ref, dfint_ref, *rest):
    count = len(SHIFTS)
    outs, (buffer, in_sem, out_sem) = rest[:count], rest[count:]
    here, core = (scalars_ref[scalars_ref.shape[0] - n] for n in (4, 1))
    for n, shift in enumerate(SHIFTS):
        target = lax.rem(here + shift, BLOCKS)
        pair = (target * CORES + (core ^ flip)) * CORES + which
        for j, slot in enumerate(block_slots(scalars_ref, pair, here, quarter, dom)):
            row = jnp.clip(scalars_ref[pair * dom + slot] - here * quarter, 0, quarter - 1)
            for t in range(dom):
                column = scalars_ref[pair * dom + t]
                pltpu.make_async_copy(
                    dfint_ref.at[
                        0,
                        pl.ds(pl.multiple_of(row * TB, TB), TB),
                        pl.ds(pl.multiple_of(column * TB, TB), TB),
                    ],
                    buffer.at[n, j, :, pl.ds(t * TB, TB)],
                    in_sem.at[n],
                ).start()
    for n in range(count):
        pltpu.make_async_copy(buffer.at[n], buffer.at[n], in_sem.at[n]).wait()
        pltpu.make_async_copy(buffer.at[n], outs[n], out_sem.at[n]).start()
    for n in range(count):
        pltpu.make_async_copy(buffer.at[n], outs[n], out_sem.at[n]).wait()


def pack(dfint, scalars, which, flip, quarter, dom):
    count = len(SHIFTS)
    tile_rows = (SLOTS, TB, dom * TB)
    return pl.pallas_call(
        functools.partial(pack_kernel, quarter, dom, which, flip),
        out_shape=[jax.ShapeDtypeStruct(tile_rows, BF16)] * count,
        grid_spec=pltpu.PrefetchScalarGridSpec(
            num_scalar_prefetch=1,
            grid=(1,),
            in_specs=[pl.BlockSpec(memory_space=pl.ANY)],
            out_specs=[pl.BlockSpec(memory_space=pl.ANY)] * count,
            scratch_shapes=[
                pltpu.VMEM((count,) + tile_rows, BF16),
                pltpu.SemaphoreType.DMA((count,)),
                pltpu.SemaphoreType.DMA((count,)),
            ],
        ),
        compiler_params=pltpu.CompilerParams(vmem_limit_bytes=VMEM_LIMIT),
        cost_estimate=pl.CostEstimate(flops=12000000000, bytes_accessed=1, transcendentals=0),
        name="pack_tiles",
    )(scalars, dfint)


def work_kernel(quarter, dom, jobs, finish, first, scalars_ref, amp_ref, *rest):
    count = len(SHIFTS)
    slots = [(which, flip) for which, flips in jobs for flip in flips]
    before_ref, rest = (None, rest) if first else (rest[0], rest[1:])
    parts, rest = rest[: count * len(slots)], rest[count * len(slots) :]
    int_out, results, inter_out = rest[0], rest[1 : 1 + len(jobs)], rest[1 + len(jobs)]
    amp, ints, half, ladder, inter_ref, amp_sem, in_sem, out_sem, small_sem = rest[2 + len(jobs) :]
    here, core = (scalars_ref[scalars_ref.shape[0] - n] for n in (4, 1))
    chip_rows = amp_ref.shape[2]
    if not first:
        load_inter = pltpu.make_async_copy(before_ref, inter_ref, small_sem.at[0])
        load_inter.start()
    slot = 0
    for job, (which, flips) in enumerate(jobs):
        for chip in range(amp_ref.shape[0]):
            pltpu.make_async_copy(
                amp_ref.at[chip, which],
                amp.at[job, pl.ds(chip * chip_rows, chip_rows), :],
                amp_sem.at[job],
            ).start()
        pair = (here * CORES + core) * CORES + which
        for s in range(dom):
            owner = scalars_ref[pair * dom + s] // quarter
            rank = jnp.int32(0)
            for earlier in range(s):
                rank = rank + (scalars_ref[pair * dom + earlier] // quarter == owner).astype(jnp.int32)
            shift = lax.rem(here - owner + BLOCKS, BLOCKS)
            for n, flow_shift in enumerate(SHIFTS):

                @pl.when(shift == flow_shift)
                def _(n=n, rank=rank, s=s, slot=slot, flips=flips):
                    for f in range(len(flips)):
                        pltpu.make_async_copy(
                            parts[(slot + f) * count + n].at[rank],
                            ints.at[slot + f, pl.ds(s * TB, TB), :],
                            in_sem.at[slot + f],
                        ).start()

        slot += len(flips)
    rows = 2 * TB
    diagonal = lax.broadcasted_iota(jnp.int32, (rows, rows), 0) == lax.broadcasted_iota(
        jnp.int32, (rows, rows), 1
    )
    traces = []
    slot = 0
    for job, (which, flips) in enumerate(jobs):
        pltpu.make_async_copy(amp.at[job], amp.at[job], amp_sem.at[job]).wait()
        for f, flip in enumerate(flips):
            place = slot + f
            pltpu.make_async_copy(ints.at[place], ints.at[place], in_sem.at[place]).wait()
            pltpu.make_async_copy(ints.at[place], int_out.at[place], out_sem.at[place]).start()
            total = jnp.zeros((rows, rows), F32)
            for r in range(0, dom * TB, rows):
                spot = pl.ds(r, rows)
                acc = lax.dot_general(ints[place, spot, :], amp[job], NT, preferred_element_type=F32)
                half[place, spot, :] = acc.astype(BF16)
                total = total + acc[:, r : r + rows]
                if not finish:
                    pltpu.make_async_copy(
                        half.at[place, spot, :], results[job].at[f, spot, :], out_sem.at[len(slots) + job]
                    ).start()
            traces.append((which * CORES + flip, jnp.sum(jnp.where(diagonal, total, 0.0))))
        if finish:
            for r in range(0, dom * TB, rows):
                spot = pl.ds(r, rows)
                acc = None
                for place in range(slot, slot + len(flips)):
                    term = lax.dot_general(
                        ints[place, spot, :], half[place], NT, preferred_element_type=F32
                    )
                    acc = term if acc is None else acc + term
                ladder[job, spot, :] = acc
                pltpu.make_async_copy(
                    ladder.at[job, spot, :], results[job].at[spot, :], out_sem.at[len(slots) + job]
                ).start()
        slot += len(flips)
    if first:
        inter = jnp.zeros(inter_ref.shape, F32)
    else:
        load_inter.wait()
        inter = inter_ref[...]
    lane = lax.broadcasted_iota(jnp.int32, inter_ref.shape, 1)
    for place, trace in traces:
        inter = jnp.where(lane == place, trace, inter)
    inter_ref[...] = inter
    store_inter = pltpu.make_async_copy(inter_ref, inter_out, small_sem.at[1])
    store_inter.start()
    for place in range(len(slots)):
        pltpu.make_async_copy(ints.at[place], int_out.at[place], out_sem.at[place]).wait()
    for job in range(len(jobs)):
        done = ladder.at[job] if finish else half
        pltpu.make_async_copy(done, results[job], out_sem.at[len(slots) + job]).wait()
    store_inter.wait()


def work(amp, before, parts, scalars, jobs, finish, quarter, dom):
    length = amp.shape[-1]
    count = sum(len(flips) for _, flips in jobs)
    anywhere = pl.BlockSpec(memory_space=pl.ANY)
    squares = (count, length, length)
    inter_shape = (BLOCKS * CORES, TB)
    result = jax.ShapeDtypeStruct((length, length), F32) if finish else jax.ShapeDtypeStruct(squares, BF16)
    first = before is None
    operands = [amp] + ([] if first else [before]) + list(parts)
    return pl.pallas_call(
        functools.partial(work_kernel, quarter, dom, jobs, finish, first),
        out_shape=[jax.ShapeDtypeStruct(squares, BF16)]
        + [result] * len(jobs)
        + [jax.ShapeDtypeStruct(inter_shape, F32)],
        grid_spec=pltpu.PrefetchScalarGridSpec(
            num_scalar_prefetch=1,
            grid=(1,),
            in_specs=[anywhere] * len(operands),
            out_specs=[anywhere] * (2 + len(jobs)),
            scratch_shapes=[
                pltpu.VMEM((len(jobs), length, length), BF16),
                pltpu.VMEM(squares, BF16),
                pltpu.VMEM(squares, BF16),
                pltpu.VMEM((len(jobs), length, length) if finish else (1, 8, TB), F32),
                pltpu.VMEM(inter_shape, F32),
                pltpu.SemaphoreType.DMA((len(jobs),)),
                pltpu.SemaphoreType.DMA((count,)),
                pltpu.SemaphoreType.DMA((count + len(jobs),)),
                pltpu.SemaphoreType.DMA((2,)),
            ],
        ),
        compiler_params=pltpu.CompilerParams(vmem_limit_bytes=VMEM_LIMIT),
        cost_estimate=pl.CostEstimate(flops=1, bytes_accessed=1, transcendentals=0),
        name="half_and_ladder" if finish else "half_ladder",
    )(scalars, *operands)


def ladder_kernel(int_ref, half_ref, before_ref, out_ref, ints, half, total, in_sem, out_sem):
    length = total.shape[0]
    rows = length // 3
    spots = [pl.ds(r, rows) for r in range(0, length, rows)]
    load_half = pltpu.make_async_copy(half_ref.at[0], half, in_sem.at[0])
    load_half.start()
    loads = []
    for n, spot in enumerate(spots):
        loads.append(
            [
                pltpu.make_async_copy(int_ref.at[0, spot, :], ints.at[spot, :], in_sem.at[2 * n + 1]),
                pltpu.make_async_copy(before_ref.at[spot, :], total.at[spot, :], in_sem.at[2 * n + 2]),
            ]
        )
        for load in loads[-1]:
            load.start()
    load_half.wait()
    for spot, pair_of_loads in zip(spots, loads):
        for load in pair_of_loads:
            load.wait()
        total[spot, :] += lax.dot_general(
            ints[spot, :], half[...], NT, preferred_element_type=F32
        )
        pltpu.make_async_copy(total.at[spot, :], out_ref.at[spot, :], out_sem.at[0]).start()
    pltpu.make_async_copy(total, out_ref, out_sem.at[0]).wait()


def ladder(ints, half, before):
    length = before.shape[0]
    anywhere = pl.BlockSpec(memory_space=pl.ANY)
    return pl.pallas_call(
        ladder_kernel,
        out_shape=jax.ShapeDtypeStruct((length, length), F32),
        in_specs=[anywhere] * 3,
        out_specs=anywhere,
        scratch_shapes=[
            pltpu.VMEM((length, length), BF16),
            pltpu.VMEM((length, length), BF16),
            pltpu.VMEM((length, length), F32),
            pltpu.SemaphoreType.DMA((7,)),
            pltpu.SemaphoreType.DMA((1,)),
        ],
        compiler_params=pltpu.CompilerParams(vmem_limit_bytes=VMEM_LIMIT),
        cost_estimate=pl.CostEstimate(flops=1, bytes_accessed=1, transcendentals=0),
        name="ladder",
    )(ints, half, before)


def cycle_kernel(places, scalars_ref, coupling_ref, inter_ref, *rest):
    each = len(places)
    width = CORES + 1
    sources, rest = rest[: each * width], rest[each * width :]
    count = (len(rest) - 4) // 2
    outs, kept, (ints, ladder, in_sem, out_sem) = rest[:count], rest[count : 2 * count], rest[2 * count :]
    y, x, core = (scalars_ref[scalars_ref.shape[0] - n] for n in (3, 2, 1))
    rows = outs[0].shape[1]
    group = RING * rows
    loads = {}
    for which in range(each):
        for t in range(RING):
            spot = pl.ds(pl.multiple_of(lax.rem(y + t, RING) * group, group), group)
            sem = (which * RING + t) * width
            loads[which, t] = [
                pltpu.make_async_copy(
                    sources[which * width + f].at[places[which][f], spot, :],
                    ints.at[which, f, t],
                    in_sem.at[sem + f],
                )
                for f in range(CORES)
            ]
            loads[which, t].append(
                pltpu.make_async_copy(
                    sources[which * width + CORES].at[spot, :],
                    ladder.at[which, t],
                    in_sem.at[sem + CORES],
                )
            )
            for load in loads[which, t]:
                load.start()
    dressing = {}
    for which in range(each):
        for f in range(CORES):
            total = jnp.float32(0)
            for source in range(BLOCKS * CORES):
                flip = (source % CORES) ^ core ^ f
                for w in range(CORES):
                    total = total + coupling_ref[core * CORES + which, source * CORES + w] * (
                        inter_ref[source, w * CORES + flip]
                    )
            dressing[which, f] = total
    for which in range(each):
        for t in range(RING):
            for load in loads[which, t]:
                load.wait()
            for k in range(RING):
                spot = pl.ds(pl.multiple_of(lax.rem(x + k, RING) * rows, rows), rows)
                total = ladder[which, t, spot, :]
                for f in range(CORES):
                    total = total + dressing[which, f] * ints[which, f, t, spot, :].astype(F32)
                n, place = (k, t) if which == 0 else (RING + t, k)
                kept[n][place] = total.astype(kept[n].dtype)
                pltpu.make_async_copy(kept[n].at[place], outs[n].at[place], out_sem.at[n]).start()
    for n in range(count):
        pltpu.make_async_copy(kept[n], outs[n], out_sem.at[n]).wait()


def add_cycle(sums, blocks, inter, coupling, scalars):
    each = len(sums)
    length = sums[0].shape[0]
    rows = length // RING**2
    anywhere = pl.BlockSpec(memory_space=pl.ANY)
    shape = (RING, rows, length)
    dtypes = [BF16 if s else F32 for s in range(RING)] * each
    sources = []
    for ints, ladder_sum in zip(blocks, sums):
        sources += [array for array, _ in ints] + [ladder_sum]
    outs = pl.pallas_call(
        functools.partial(cycle_kernel, [[place for _, place in ints] for ints in blocks]),
        out_shape=[jax.ShapeDtypeStruct(shape, dtype) for dtype in dtypes],
        grid_spec=pltpu.PrefetchScalarGridSpec(
            num_scalar_prefetch=3,
            grid=(1,),
            in_specs=[anywhere] * len(sources),
            out_specs=[anywhere] * len(dtypes),
            scratch_shapes=[pltpu.VMEM(shape, dtype) for dtype in dtypes]
            + [
                pltpu.VMEM((each, CORES, RING, RING * rows, length), BF16),
                pltpu.VMEM((each, RING, RING * rows, length), F32),
                pltpu.SemaphoreType.DMA((each * RING * (CORES + 1),)),
                pltpu.SemaphoreType.DMA((len(dtypes),)),
            ],
        ),
        compiler_params=pltpu.CompilerParams(vmem_limit_bytes=VMEM_LIMIT),
        cost_estimate=pl.CostEstimate(flops=1, bytes_accessed=1, transcendentals=0),
        name="add_cycle",
    )(scalars, coupling, inter, *sources)
    return [outs[which * RING : (which + 1) * RING] for which in range(each)]


def sum_over(axis, parts):
    total = parts[0].astype(F32)
    for s in (2, 1, 3):
        perm = [(i, (i + s) % RING) for i in range(RING)]
        total = total + lax.ppermute(parts[s].astype(BF16), axis, perm).astype(F32)
    return total


def masked_amps(amps, pair_mask, first_row, dom):
    pairs, rows, length = amps.shape
    row_slot = (first_row + jnp.arange(rows, dtype=jnp.int32)) // TB
    slot_pick = row_slot[:, None] == jnp.arange(dom, dtype=jnp.int32)[None, :]
    row_tiles = jnp.sum(
        jnp.where(slot_pick[None, :, :, None], pair_mask[:, None, :, :], 0), axis=2
    ).astype(BF16)
    tiles = amps.reshape(pairs, rows, dom, TB) * row_tiles[:, :, :, None]
    return tiles.reshape(pairs, rows, length)


def by_core(core, mine, other, axis):
    return jnp.where(
        core == 0,
        jnp.concatenate([mine, other], axis=axis),
        jnp.concatenate([other, mine], axis=axis),
    )


def make_body(ny, nx):
    def send(key, packed):
        return [
            part if (s, key[1]) == (0, 0) else hop(s, key[1])(part)
            for s, part in zip(SHIFTS, packed)
        ]

    def body(amps, domain, pair_mask, dfint, coupling):
        pairs, own, length = amps.shape
        dom = domain.shape[1]
        quarter = dfint.shape[1] // TB
        each = pairs // CORES
        chips = ny * nx
        z, y, x, c = (lax.axis_index(name).astype(jnp.int32) for name in ("z", "y", "x", "c"))
        scalars = jnp.concatenate([domain.reshape(-1), jnp.stack([z, y, x, c])])
        order = [(which, f) for which in range(each) for f in range(CORES)]
        packed = {order[0]: pack(dfint, scalars, *order[0], quarter, dom)}
        for key in order[1:]:
            packed[key] = pack(dfint, scalars, *key, quarter, dom)
        (packed[1, 0], amps, pair_mask) = lax.optimization_barrier((packed[1, 0], amps, pair_mask))
        masked = masked_amps(amps, pair_mask, ((y * nx + x) * CORES + c) * own, dom)
        mine = lax.dynamic_slice_in_dim(masked, c * each, each, axis=0)
        other = swap_cores(lax.dynamic_slice_in_dim(masked, (1 - c) * each, each, axis=0))
        both = by_core(c, mine, other, 1)
        amp = lax.all_to_all(
            jnp.broadcast_to(both[None], (chips,) + both.shape), ("y", "x"), 0, 0, tiled=True
        )
        parts = {key: send(key, packed[key]) for key in order[:-1]}
        parts[order[-1]] = send(order[-1], packed[order[-1]])
        ints, ladder0, ladder1, inter = work(
            amp,
            None,
            parts[0, 0] + parts[0, 1] + parts[1, 0],
            scalars,
            ((0, (0, 1)), (1, (0,))),
            True,
            quarter,
            dom,
        )
        late, half, inter = work(
            amp, inter, parts[1, 1], scalars, ((1, (1,)),), False, quarter, dom
        )
        sums = [ladder0, ladder(late, half, ladder1)]
        blocks = [[(ints, 0), (ints, 1)], [(ints, 2), (late, 0)]]
        every = lax.all_to_all(inter, ("z", "c"), 0, 0, tiled=True)
        ends = []
        for ordered, (first, second) in zip(
            add_cycle(sums, blocks, every, coupling, scalars), (("x", "y"), ("y", "x"))
        ):
            stage = sum_over(first, ordered)
            ends.append(sum_over(second, [stage[s] for s in range(RING)]))
        result = jnp.stack(ends).astype(BF16)
        mine = lax.dynamic_slice_in_dim(result, c * own, own, axis=1)
        other = swap_cores(lax.dynamic_slice_in_dim(result, (1 - c) * own, own, axis=1))
        return by_core(c, mine, other, 0)

    return body


def solution(mesh):
    ny = nx = 4
    grid = Mesh(mesh.devices.reshape(BLOCKS, ny, nx, CORES), ("z", "y", "x", "c"))
    virt = ("y", "x", "c")
    return jax.shard_map(
        make_body(ny, nx),
        mesh=grid,
        in_specs=(P("z", virt, None), P(), P("z", None, None), P(virt, "z", None), P("z", None)),
        out_specs=P("z", virt, None),
        check_vma=False,
    )
```

```python
import functools

import jax
import jax.numpy as jnp
from jax import lax
from jax.experimental import pallas as pl
from jax.experimental.pallas import tpu as pltpu
from jax.sharding import Mesh
from jax.sharding import PartitionSpec as P

TB = 128
BLOCKS = 4
RING = 4
CORES = 2
SLOTS = 2
VMEM_LIMIT = 52 * 2**20
BF16 = jnp.bfloat16
F32 = jnp.float32
NT = (((1,), (1,)), ((), ()))
SHIFTS = (1, 3, 2, 0)


def hop(shift, flip):
    perm = [
        (z * CORES + c, (z + shift) % BLOCKS * CORES + (c ^ flip))
        for z in range(BLOCKS)
        for c in range(CORES)
    ]
    return functools.partial(lax.ppermute, axis_name=("z", "c"), perm=perm)


def swap_cores(value):
    return lax.ppermute(value, "c", [(0, 1), (1, 0)])


def block_slots(scalars_ref, pair, block, quarter, dom):
    found = jnp.int32(0)
    first = jnp.int32(0)
    second = jnp.int32(0)
    for s in range(dom):
        inside = scalars_ref[pair * dom + s] // quarter == block
        first = jnp.where(inside & (found == 0), s, first)
        second = jnp.where(inside & (found == 1), s, second)
        found = found + inside.astype(jnp.int32)
    return first, second


def pack_kernel(quarter, dom, which, flip, scalars_ref, dfint_ref, *rest):
    count = len(SHIFTS)
    outs, (buffer, in_sem, out_sem) = rest[:count], rest[count:]
    here, core = (scalars_ref[scalars_ref.shape[0] - n] for n in (4, 1))
    for n, shift in enumerate(SHIFTS):
        target = lax.rem(here + shift, BLOCKS)
        pair = (target * CORES + (core ^ flip)) * CORES + which
        for j, slot in enumerate(block_slots(scalars_ref, pair, here, quarter, dom)):
            row = jnp.clip(scalars_ref[pair * dom + slot] - here * quarter, 0, quarter - 1)
            for t in range(dom):
                column = scalars_ref[pair * dom + t]
                pltpu.make_async_copy(
                    dfint_ref.at[
                        0,
                        pl.ds(pl.multiple_of(row * TB, TB), TB),
                        pl.ds(pl.multiple_of(column * TB, TB), TB),
                    ],
                    buffer.at[n, j, :, pl.ds(t * TB, TB)],
                    in_sem.at[n],
                ).start()
    for n in range(count):
        pltpu.make_async_copy(buffer.at[n], buffer.at[n], in_sem.at[n]).wait()
        pltpu.make_async_copy(buffer.at[n], outs[n], out_sem.at[n]).start()
    for n in range(count):
        pltpu.make_async_copy(buffer.at[n], outs[n], out_sem.at[n]).wait()


def pack(dfint, scalars, which, flip, quarter, dom):
    count = len(SHIFTS)
    tile_rows = (SLOTS, TB, dom * TB)
    return pl.pallas_call(
        functools.partial(pack_kernel, quarter, dom, which, flip),
        out_shape=[jax.ShapeDtypeStruct(tile_rows, BF16)] * count,
        grid_spec=pltpu.PrefetchScalarGridSpec(
            num_scalar_prefetch=1,
            grid=(1,),
            in_specs=[pl.BlockSpec(memory_space=pl.ANY)],
            out_specs=[pl.BlockSpec(memory_space=pl.ANY)] * count,
            scratch_shapes=[
                pltpu.VMEM((count,) + tile_rows, BF16),
                pltpu.SemaphoreType.DMA((count,)),
                pltpu.SemaphoreType.DMA((count,)),
            ],
        ),
        compiler_params=pltpu.CompilerParams(vmem_limit_bytes=VMEM_LIMIT),
        cost_estimate=pl.CostEstimate(flops=12000000000, bytes_accessed=1, transcendentals=0),
        name="pack_tiles",
    )(scalars, dfint)


def work_kernel(quarter, dom, jobs, finish, first, scalars_ref, amp_ref, *rest):
    count = len(SHIFTS)
    slots = [(which, flip) for which, flips in jobs for flip in flips]
    before_ref, rest = (None, rest) if first else (rest[0], rest[1:])
    parts, rest = rest[: count * len(slots)], rest[count * len(slots) :]
    int_out, results, inter_out = rest[0], rest[1 : 1 + len(jobs)], rest[1 + len(jobs)]
    amp, ints, half, ladder, inter_ref, amp_sem, in_sem, out_sem, small_sem = rest[2 + len(jobs) :]
    here, core = (scalars_ref[scalars_ref.shape[0] - n] for n in (4, 1))
    chip_rows = amp_ref.shape[2]
    if not first:
        load_inter = pltpu.make_async_copy(before_ref, inter_ref, small_sem.at[0])
        load_inter.start()
    slot = 0
    for job, (which, flips) in enumerate(jobs):
        for chip in range(amp_ref.shape[0]):
            pltpu.make_async_copy(
                amp_ref.at[chip, which],
                amp.at[job, pl.ds(chip * chip_rows, chip_rows), :],
                amp_sem.at[job],
            ).start()
        pair = (here * CORES + core) * CORES + which
        for s in range(dom):
            owner = scalars_ref[pair * dom + s] // quarter
            rank = jnp.int32(0)
            for earlier in range(s):
                rank = rank + (scalars_ref[pair * dom + earlier] // quarter == owner).astype(jnp.int32)
            shift = lax.rem(here - owner + BLOCKS, BLOCKS)
            for n, flow_shift in enumerate(SHIFTS):

                @pl.when(shift == flow_shift)
                def _(n=n, rank=rank, s=s, slot=slot, flips=flips):
                    for f in range(len(flips)):
                        pltpu.make_async_copy(
                            parts[(slot + f) * count + n].at[rank],
                            ints.at[slot + f, pl.ds(s * TB, TB), :],
                            in_sem.at[slot + f],
                        ).start()

        slot += len(flips)
    rows = 2 * TB
    diagonal = lax.broadcasted_iota(jnp.int32, (rows, rows), 0) == lax.broadcasted_iota(
        jnp.int32, (rows, rows), 1
    )
    traces = []
    slot = 0
    for job, (which, flips) in enumerate(jobs):
        pltpu.make_async_copy(amp.at[job], amp.at[job], amp_sem.at[job]).wait()
        for f, flip in enumerate(flips):
            place = slot + f
            pltpu.make_async_copy(ints.at[place], ints.at[place], in_sem.at[place]).wait()
            pltpu.make_async_copy(ints.at[place], int_out.at[place], out_sem.at[place]).start()
            total = jnp.zeros((rows, rows), F32)
            for r in range(0, dom * TB, rows):
                spot = pl.ds(r, rows)
                acc = lax.dot_general(ints[place, spot, :], amp[job], NT, preferred_element_type=F32)
                half[place, spot, :] = acc.astype(BF16)
                total = total + acc[:, r : r + rows]
                if not finish:
                    pltpu.make_async_copy(
                        half.at[place, spot, :], results[job].at[f, spot, :], out_sem.at[len(slots) + job]
                    ).start()
            traces.append((which * CORES + flip, jnp.sum(jnp.where(diagonal, total, 0.0))))
        if finish:
            for r in range(0, dom * TB, rows):
                spot = pl.ds(r, rows)
                acc = None
                for place in range(slot, slot + len(flips)):
                    term = lax.dot_general(
                        ints[place, spot, :], half[place], NT, preferred_element_type=F32
                    )
                    acc = term if acc is None else acc + term
                ladder[job, spot, :] = acc
                pltpu.make_async_copy(
                    ladder.at[job, spot, :], results[job].at[spot, :], out_sem.at[len(slots) + job]
                ).start()
        slot += len(flips)
    if first:
        inter = jnp.zeros(inter_ref.shape, F32)
    else:
        load_inter.wait()
        inter = inter_ref[...]
    lane = lax.broadcasted_iota(jnp.int32, inter_ref.shape, 1)
    for place, trace in traces:
        inter = jnp.where(lane == place, trace, inter)
    inter_ref[...] = inter
    store_inter = pltpu.make_async_copy(inter_ref, inter_out, small_sem.at[1])
    store_inter.start()
    for place in range(len(slots)):
        pltpu.make_async_copy(ints.at[place], int_out.at[place], out_sem.at[place]).wait()
    for job in range(len(jobs)):
        done = ladder.at[job] if finish else half
        pltpu.make_async_copy(done, results[job], out_sem.at[len(slots) + job]).wait()
    store_inter.wait()


def work(amp, before, parts, scalars, jobs, finish, quarter, dom):
    length = amp.shape[-1]
    count = sum(len(flips) for _, flips in jobs)
    anywhere = pl.BlockSpec(memory_space=pl.ANY)
    squares = (count, length, length)
    inter_shape = (BLOCKS * CORES, TB)
    result = jax.ShapeDtypeStruct((length, length), F32) if finish else jax.ShapeDtypeStruct(squares, BF16)
    first = before is None
    operands = [amp] + ([] if first else [before]) + list(parts)
    return pl.pallas_call(
        functools.partial(work_kernel, quarter, dom, jobs, finish, first),
        out_shape=[jax.ShapeDtypeStruct(squares, BF16)]
        + [result] * len(jobs)
        + [jax.ShapeDtypeStruct(inter_shape, F32)],
        grid_spec=pltpu.PrefetchScalarGridSpec(
            num_scalar_prefetch=1,
            grid=(1,),
            in_specs=[anywhere] * len(operands),
            out_specs=[anywhere] * (2 + len(jobs)),
            scratch_shapes=[
                pltpu.VMEM((len(jobs), length, length), BF16),
                pltpu.VMEM(squares, BF16),
                pltpu.VMEM(squares, BF16),
                pltpu.VMEM((len(jobs), length, length) if finish else (1, 8, TB), F32),
                pltpu.VMEM(inter_shape, F32),
                pltpu.SemaphoreType.DMA((len(jobs),)),
                pltpu.SemaphoreType.DMA((count,)),
                pltpu.SemaphoreType.DMA((count + len(jobs),)),
                pltpu.SemaphoreType.DMA((2,)),
            ],
        ),
        compiler_params=pltpu.CompilerParams(vmem_limit_bytes=VMEM_LIMIT),
        cost_estimate=pl.CostEstimate(flops=1, bytes_accessed=1, transcendentals=0),
        name="half_and_ladder" if finish else "half_ladder",
    )(scalars, *operands)


def ladder_kernel(int_ref, half_ref, before_ref, out_ref, ints, half, total, in_sem, out_sem):
    length = total.shape[0]
    rows = length // 3
    spots = [pl.ds(r, rows) for r in range(0, length, rows)]
    load_half = pltpu.make_async_copy(half_ref.at[0], half, in_sem.at[0])
    load_half.start()
    loads = []
    for n, spot in enumerate(spots):
        loads.append(
            [
                pltpu.make_async_copy(int_ref.at[0, spot, :], ints.at[spot, :], in_sem.at[2 * n + 1]),
                pltpu.make_async_copy(before_ref.at[spot, :], total.at[spot, :], in_sem.at[2 * n + 2]),
            ]
        )
        for load in loads[-1]:
            load.start()
    load_half.wait()
    for spot, pair_of_loads in zip(spots, loads):
        for load in pair_of_loads:
            load.wait()
        total[spot, :] += lax.dot_general(
            ints[spot, :], half[...], NT, preferred_element_type=F32
        )
        pltpu.make_async_copy(total.at[spot, :], out_ref.at[spot, :], out_sem.at[0]).start()
    pltpu.make_async_copy(total, out_ref, out_sem.at[0]).wait()


def ladder(ints, half, before):
    length = before.shape[0]
    anywhere = pl.BlockSpec(memory_space=pl.ANY)
    return pl.pallas_call(
        ladder_kernel,
        out_shape=jax.ShapeDtypeStruct((length, length), F32),
        in_specs=[anywhere] * 3,
        out_specs=anywhere,
        scratch_shapes=[
            pltpu.VMEM((length, length), BF16),
            pltpu.VMEM((length, length), BF16),
            pltpu.VMEM((length, length), F32),
            pltpu.SemaphoreType.DMA((7,)),
            pltpu.SemaphoreType.DMA((1,)),
        ],
        compiler_params=pltpu.CompilerParams(vmem_limit_bytes=VMEM_LIMIT),
        cost_estimate=pl.CostEstimate(flops=1, bytes_accessed=1, transcendentals=0),
        name="ladder",
    )(ints, half, before)


def cycle_kernel(places, scalars_ref, coupling_ref, inter_ref, *rest):
    each = len(places)
    width = CORES + 1
    sources, rest = rest[: each * width], rest[each * width :]
    count = (len(rest) - 4) // 2
    outs, kept, (ints, ladder, in_sem, out_sem) = rest[:count], rest[count : 2 * count], rest[2 * count :]
    y, x, core = (scalars_ref[scalars_ref.shape[0] - n] for n in (3, 2, 1))
    rows = outs[0].shape[1]
    group = RING * rows
    loads = {}
    for which in range(each):
        for t in range(RING):
            spot = pl.ds(pl.multiple_of(lax.rem(y + t, RING) * group, group), group)
            sem = (which * RING + t) * width
            loads[which, t] = [
                pltpu.make_async_copy(
                    sources[which * width + f].at[places[which][f], spot, :],
                    ints.at[which, f, t],
                    in_sem.at[sem + f],
                )
                for f in range(CORES)
            ]
            loads[which, t].append(
                pltpu.make_async_copy(
                    sources[which * width + CORES].at[spot, :],
                    ladder.at[which, t],
                    in_sem.at[sem + CORES],
                )
            )
            for load in loads[which, t]:
                load.start()
    dressing = {}
    for which in range(each):
        for f in range(CORES):
            total = jnp.float32(0)
            for source in range(BLOCKS * CORES):
                flip = (source % CORES) ^ core ^ f
                for w in range(CORES):
                    total = total + coupling_ref[core * CORES + which, source * CORES + w] * (
                        inter_ref[source, w * CORES + flip]
                    )
            dressing[which, f] = total
    for which in range(each):
        for t in range(RING):
            for load in loads[which, t]:
                load.wait()
            for k in range(RING):
                spot = pl.ds(pl.multiple_of(lax.rem(x + k, RING) * rows, rows), rows)
                total = ladder[which, t, spot, :]
                for f in range(CORES):
                    total = total + dressing[which, f] * ints[which, f, t, spot, :].astype(F32)
                n, place = (k, t) if which == 0 else (RING + t, k)
                kept[n][place] = total.astype(kept[n].dtype)
                pltpu.make_async_copy(kept[n].at[place], outs[n].at[place], out_sem.at[n]).start()
    for n in range(count):
        pltpu.make_async_copy(kept[n], outs[n], out_sem.at[n]).wait()


def add_cycle(sums, blocks, inter, coupling, scalars):
    each = len(sums)
    length = sums[0].shape[0]
    rows = length // RING**2
    anywhere = pl.BlockSpec(memory_space=pl.ANY)
    shape = (RING, rows, length)
    dtypes = [BF16 if s else F32 for s in range(RING)] * each
    sources = []
    for ints, ladder_sum in zip(blocks, sums):
        sources += [array for array, _ in ints] + [ladder_sum]
    outs = pl.pallas_call(
        functools.partial(cycle_kernel, [[place for _, place in ints] for ints in blocks]),
        out_shape=[jax.ShapeDtypeStruct(shape, dtype) for dtype in dtypes],
        grid_spec=pltpu.PrefetchScalarGridSpec(
            num_scalar_prefetch=3,
            grid=(1,),
            in_specs=[anywhere] * len(sources),
            out_specs=[anywhere] * len(dtypes),
            scratch_shapes=[pltpu.VMEM(shape, dtype) for dtype in dtypes]
            + [
                pltpu.VMEM((each, CORES, RING, RING * rows, length), BF16),
                pltpu.VMEM((each, RING, RING * rows, length), F32),
                pltpu.SemaphoreType.DMA((each * RING * (CORES + 1),)),
                pltpu.SemaphoreType.DMA((len(dtypes),)),
            ],
        ),
        compiler_params=pltpu.CompilerParams(vmem_limit_bytes=VMEM_LIMIT),
        cost_estimate=pl.CostEstimate(flops=1, bytes_accessed=1, transcendentals=0),
        name="add_cycle",
    )(scalars, coupling, inter, *sources)
    return [outs[which * RING : (which + 1) * RING] for which in range(each)]


def sum_over(axis, parts):
    total = parts[0].astype(F32)
    for s in (2, 1, 3):
        perm = [(i, (i + s) % RING) for i in range(RING)]
        total = total + lax.ppermute(parts[s].astype(BF16), axis, perm).astype(F32)
    return total


def masked_amps(amps, pair_mask, first_row, dom):
    pairs, rows, length = amps.shape
    row_slot = (first_row + jnp.arange(rows, dtype=jnp.int32)) // TB
    slot_pick = row_slot[:, None] == jnp.arange(dom, dtype=jnp.int32)[None, :]
    row_tiles = jnp.sum(
        jnp.where(slot_pick[None, :, :, None], pair_mask[:, None, :, :], 0), axis=2
    ).astype(BF16)
    tiles = amps.reshape(pairs, rows, dom, TB) * row_tiles[:, :, :, None]
    return tiles.reshape(pairs, rows, length)


def by_core(core, mine, other, axis):
    return jnp.where(
        core == 0,
        jnp.concatenate([mine, other], axis=axis),
        jnp.concatenate([other, mine], axis=axis),
    )


def make_body(ny, nx):
    def send(key, packed):
        return [
            part if (s, key[1]) == (0, 0) else hop(s, key[1])(part)
            for s, part in zip(SHIFTS, packed)
        ]

    def body(amps, domain, pair_mask, dfint, coupling):
        pairs, own, length = amps.shape
        dom = domain.shape[1]
        quarter = dfint.shape[1] // TB
        each = pairs // CORES
        chips = ny * nx
        z, y, x, c = (lax.axis_index(name).astype(jnp.int32) for name in ("z", "y", "x", "c"))
        scalars = jnp.concatenate([domain.reshape(-1), jnp.stack([z, y, x, c])])
        order = [(which, f) for which in range(each) for f in range(CORES)]
        packed = {order[0]: pack(dfint, scalars, *order[0], quarter, dom)}
        for key in order[1:]:
            packed[key] = pack(dfint, scalars, *key, quarter, dom)
        (packed[1, 0], amps, pair_mask) = lax.optimization_barrier((packed[1, 0], amps, pair_mask))
        masked = masked_amps(amps, pair_mask, ((y * nx + x) * CORES + c) * own, dom)
        mine = lax.dynamic_slice_in_dim(masked, c * each, each, axis=0)
        other = swap_cores(lax.dynamic_slice_in_dim(masked, (1 - c) * each, each, axis=0))
        both = by_core(c, mine, other, 1)
        amp = lax.all_to_all(
            jnp.broadcast_to(both[None], (chips,) + both.shape), ("y", "x"), 0, 0, tiled=True
        )
        parts = {key: send(key, packed[key]) for key in order[:-1]}
        parts[order[-1]] = send(order[-1], packed[order[-1]])
        ints, ladder0, ladder1, inter = work(
            amp,
            None,
            parts[0, 0] + parts[0, 1] + parts[1, 0],
            scalars,
            ((0, (0, 1)), (1, (0,))),
            True,
            quarter,
            dom,
        )
        late, half, inter = work(
            amp, inter, parts[1, 1], scalars, ((1, (1,)),), False, quarter, dom
        )
        sums = [ladder0, ladder(late, half, ladder1)]
        blocks = [[(ints, 0), (ints, 1)], [(ints, 2), (late, 0)]]
        every = lax.all_to_all(inter, ("z", "c"), 0, 0, tiled=True)
        ends = []
        for ordered, (first, second) in zip(
            add_cycle(sums, blocks, every, coupling, scalars), (("x", "y"), ("y", "x"))
        ):
            stage = sum_over(first, ordered)
            ends.append(sum_over(second, [stage[s] for s in range(RING)]))
        result = jnp.stack(ends).astype(BF16)
        mine = lax.dynamic_slice_in_dim(result, c * own, own, axis=1)
        other = swap_cores(lax.dynamic_slice_in_dim(result, (1 - c) * own, own, axis=1))
        return by_core(c, mine, other, 0)

    return body


def solution(mesh):
    ny = nx = 4
    grid = Mesh(mesh.devices.reshape(BLOCKS, ny, nx, CORES), ("z", "y", "x", "c"))
    virt = ("y", "x", "c")
    return jax.shard_map(
        make_body(ny, nx),
        mesh=grid,
        in_specs=(P("z", virt, None), P(), P("z", None, None), P(virt, "z", None), P("z", None)),
        out_specs=P("z", virt, None),
        check_vma=False,
    )
```
